1024 devices in a mesh: ax: 32 (over y_lo, x), circ: 32 (over z, y_hi, core).
Axes of the slice: x: 8, y: 8 (y_hi: 2, y_lo: 4; y = y_hi * 4 + y_lo), z: 8, core: 2. Of those that a mesh axis runs over, the one named last changes fastest.
Arguments:
- cotangent: float32 [16, 128, 4096], P(None, 'ax', 'circ'), may hold values from -6 to 6
- off_blocks: bfloat16 [8, 16, 16, 128, 4096], P(None, None, None, 'ax', 'circ'), may hold values from -0.375 to 0.375
- diag_inverse: bfloat16 [16, 16, 128, 4096], P(None, None, 'ax', 'circ'), may hold values from -1 to 1.6015625, as said below
Outputs:
- grad_source: float32 [16, 128, 4096], P(None, 'ax', 'circ')
- grad_initial: float32 [16, 128, 4096], P(None, 'ax', 'circ')
The draws below stay inside these ranges and needn't reach their ends.
Inputs may be any that keep to these rules, and one draw needn't show every extreme that they name: `diag_inverse`: each cell's block has diagonal entries of 0.6 to about 1.6 and small signed entries elsewhere.
All inputs are finite; a program needn't handle non-finite values.
Results may differ from the reference program's by a relative error of at most 0.0003.
Values may be sent and summed in bfloat16 or wider, within the bound.
A program may use at most 64 MiB of HBM per device.

```python
import jax
import jax.numpy as jnp
from jax import lax

RADIAL = 16
STEPS = 4
NA = 128
NC = 4096


def draw_diag_inverse(key, part):
    first_key, second_key = jax.random.split(jax.random.fold_in(key, 11))
    main = jax.random.uniform(first_key, (RADIAL, NA, NC), jnp.float32, 0.6, 1.6)
    spread = jnp.clip(0.075 * jax.random.normal(second_key, (RADIAL, RADIAL, NA, NC), jnp.float32), -0.45, 0.45)
    unit = jnp.eye(RADIAL, dtype=jnp.float32)[:, :, None, None]
    return (unit * main[:, None, :, :] + (1.0 - unit) * spread).astype(jnp.bfloat16)


def steps_of(stream_key, extent, cuts, smallest, top_value):
    factor_of, own = 1.0, jax.random.fold_in(stream_key, 6)
    for position, parts in cuts:
        steps = jnp.exp(jax.random.uniform(jax.random.fold_in(own, position), (parts,), jnp.float32, smallest / len(cuts), top_value / len(cuts)))
        factor_of = factor_of * jnp.repeat(steps, extent[position] // parts).reshape([-1 if axis == position else 1 for axis in range(len(extent))])
    return factor_of


def centred(rng, dims, scale, most, pieces=(), held_as=jnp.bfloat16):
    result = jax.random.normal(rng, dims, jnp.float32) * scale
    if len(pieces) > 0:
        result = steps_of(rng, dims, pieces, -0.22, 0.18) * result
    return jnp.clip(result, min=-most, max=most).astype(held_as)


def setup_inputs(seed: int = 0) -> dict:
    arg_keys = jax.random.split(jax.random.key(seed), 4)
    return {
        "cotangent": centred(arg_keys[0], (RADIAL, NA, NC), 1.0, 6.0, ((1, 32), (2, 32)), jnp.float32),
        "off_blocks": centred(arg_keys[1], (8, RADIAL, RADIAL, NA, NC), (16 * RADIAL) ** -0.5, 0.375, ((3, 32), (4, 32))),
        "diag_inverse": draw_diag_inverse(jax.random.fold_in(arg_keys[3], 71), 0),
    }


OFFSETS = ((-1, -1), (-1, 0), (-1, 1), (0, -1), (0, 1), (1, -1), (1, 0), (1, 1))


def transposed(off_blocks, weighted):
    total = jnp.zeros(weighted.shape, jnp.float32)
    zero_row = jnp.zeros((weighted.shape[0], 1, weighted.shape[2]), jnp.float32)
    for slot in range(8):
        shift_a, shift_c = OFFSETS[slot]
        moved = jnp.einsum('rsac,rac->sac', off_blocks[slot].astype(jnp.float32), weighted, precision=lax.Precision.HIGHEST)
        moved = jnp.roll(moved, shift_c, axis=2)
        if shift_a == 1:
            moved = jnp.concatenate([zero_row, moved[:, :-1]], axis=1)
        elif shift_a == -1:
            moved = jnp.concatenate([moved[:, 1:], zero_row], axis=1)
        total = total + moved
    return total


def reference(cotangent, off_blocks, diag_inverse):
    adjoint = cotangent
    grad_source = jnp.zeros(cotangent.shape, jnp.float32)
    for step in range(STEPS):
        weighted = jnp.einsum('rsac,rac->sac', diag_inverse.astype(jnp.float32), adjoint, precision=lax.Precision.HIGHEST)
        grad_source = grad_source + weighted
        adjoint = -transposed(off_blocks, weighted)
    return grad_source, adjoint
```

```python
import functools

import jax
import jax.numpy as jnp
from jax import lax
from jax.experimental import pallas as pl
from jax.experimental.pallas import tpu as pltpu
from jax.sharding import PartitionSpec as P

STEPS = 4
MESH = pl.DeviceIdType.MESH
F32 = jnp.float32
BF16 = jnp.bfloat16


def halves(field):
    sub = lax.broadcasted_iota(jnp.int32, (8, 128), 0)
    out = []
    for v in range(8):
        here = field[8 * v : 8 * v + 8]
        turned = pltpu.roll(here, 4, 0)
        out.append(jnp.where(sub < 4, here, turned))
        out.append(jnp.where(sub < 4, turned, here))
    return out


def spread(field):
    sub = lax.broadcasted_iota(jnp.int32, (8, 128), 0)
    group = lax.broadcasted_iota(jnp.int32, (8, 128), 1) >> 3
    total = jnp.zeros((8, 128), F32)
    for v in range(8):
        total = jnp.where(group == 2 * v + (sub >> 2), field[8 * v : 8 * v + 8], total)
    return total + pltpu.roll(total, 4, 0)


def split(x, parts):
    out = []
    for _ in range(parts):
        part = x.astype(BF16)
        out.append(part)
        x = x - part.astype(F32)
    return out


def times(blocks, rows):
    return (blocks.reshape(8, 8, 128) * rows[None]).reshape(64, 128)


def kernel(
    cot,
    off,
    diag,
    source_out,
    initial_out,
    av,
    bv,
    dv,
    source,
    ghost_b,
    ghost_d,
    out_b,
    in_b,
    out_a,
    in_a,
    pk,
    up_s,
    down_s,
    q,
    ax_out,
    ax_in,
    pick,
    same,
    moves,
    load_sem,
    store_sem,
    gsend,
    grecv,
    asend,
    arecv,
):
    ax, circ = lax.axis_index("ax"), lax.axis_index("circ")
    n_ax, n_circ = lax.axis_size("ax"), lax.axis_size("circ")
    right = (ax, lax.rem(circ + 1, n_circ))
    left = (ax, lax.rem(circ + n_circ - 1, n_circ))
    above, below = (ax - 1, circ), (ax + 1, circ)
    has_above, has_below = ax > 0, ax < n_ax - 1

    loads = [
        pltpu.make_async_copy(cot, av, load_sem.at[8]),
        pltpu.make_async_copy(diag, dv, load_sem.at[9]),
    ]
    for copy in loads:
        copy.start()

    def load(k):
        return pltpu.make_async_copy(off.at[k], bv.at[k], load_sem.at[k])

    for k in range(8):
        load(k).start()

    @pl.when(jnp.logical_not(has_above))
    def _():
        ax_in[:, 0] = jnp.zeros((STEPS, 32, 128), F32)

    @pl.when(jnp.logical_not(has_below))
    def _():
        ax_in[:, 1] = jnp.zeros((STEPS, 32, 128), F32)

    barrier = pltpu.get_barrier_semaphore()
    pl.semaphore_signal(barrier, inc=1, device_id=right, device_id_type=MESH)
    pl.semaphore_signal(barrier, inc=1, device_id=left, device_id_type=MESH)

    @pl.when(has_above)
    def _():
        pl.semaphore_signal(barrier, inc=1, device_id=above, device_id_type=MESH)

    @pl.when(has_below)
    def _():
        pl.semaphore_signal(barrier, inc=1, device_id=below, device_id_type=MESH)

    row = lax.broadcasted_iota(jnp.int32, (256, 128), 0)
    col = lax.broadcasted_iota(jnp.int32, (256, 128), 1)
    edge = ((row + 4) & 127) == (col & 7)
    pick[...] = jnp.where(edge & (((col >> 3) & 1) == (row >> 7)), 1.0, 0.0).astype(BF16)
    same[0] = jnp.where((row & 7) == (col & 7), 1.0, 0.0).astype(BF16)
    same[1] = jnp.where(edge, 1.0, 0.0).astype(BF16)
    g_from, g_to = row & 7, col & 7
    for i, shift in enumerate((-1, 0, 1)):
        inside = g_to == g_from + shift
        if shift == 1:
            inside = inside & (g_from != 3)
            outside = (g_from == 3) & (col == 0)
        elif shift == -1:
            inside = inside & (g_from != 4)
            outside = (g_from == 4) & (col == 127)
        moves[i, :, 128:] = jnp.where(inside, 1.0, 0.0).astype(BF16)
        if shift == 0:
            moves[i, :, :128] = jnp.zeros((256, 128), BF16)
        else:
            moves[i, :, :128] = jnp.where(outside, 1.0, 0.0).astype(BF16)

    lane = lax.broadcasted_iota(jnp.int32, (64, 128), 1)
    sub = lax.broadcasted_iota(jnp.int32, (64, 128), 0)
    ghost = lane & 7

    def pick_edges(blocks):
        both = jnp.concatenate(
            [blocks[:, 0].reshape(512, 128), blocks[:, 1].reshape(512, 128)], axis=1
        )
        found = jnp.dot(both, pick[...], preferred_element_type=F32)
        total = found[0:64]
        for p in range(1, 8):
            total = jnp.where((lane >> 4) == p, found[64 * p : 64 * p + 64], total)
        return total

    loads[0].wait()
    field = av[...]
    copies = [
        jnp.dot(part, same[1, :128], preferred_element_type=F32) for part in split(field, 3)
    ]
    out_a[...] = spread(copies[0] + copies[1] + copies[2])
    loads[1].wait()
    edges = pick_edges(dv[...]).astype(BF16)
    out_b[0, 4] = edges
    out_b[1, 4] = edges

    @pl.loop(0, 4)
    def _(pair):
        load(2 * pair).wait()
        first = pick_edges(bv[2 * pair])
        load(2 * pair + 1).wait()
        second = pick_edges(bv[2 * pair + 1])
        out_b[0, pair] = jnp.where(ghost < 4, first, pltpu.roll(second, 4, 1)).astype(BF16)
        out_b[1, pair] = jnp.where(ghost < 4, pltpu.roll(first, 124, 1), second).astype(BF16)

    pl.semaphore_wait(
        barrier, 2 + has_above.astype(jnp.int32) + has_below.astype(jnp.int32)
    )

    ghosts = []
    for side, target in ((0, right), (1, left)):
        ghosts.append(
            pltpu.make_async_remote_copy(
                src_ref=out_b.at[side],
                dst_ref=in_b.at[side],
                send_sem=gsend.at[side],
                recv_sem=grecv.at[side],
                device_id=target,
                device_id_type=MESH,
            )
        )
        ghosts.append(
            pltpu.make_async_remote_copy(
                src_ref=out_a,
                dst_ref=in_a.at[side],
                send_sem=gsend.at[2 + side],
                recv_sem=grecv.at[2 + side],
                device_id=target,
                device_id_type=MESH,
            )
        )
    for copy in ghosts:
        copy.start()

    def weigh(a, first):
        rows = halves(a)
        w = jnp.zeros((64, 128), F32)
        for r in range(16):
            w = w + times(dv[r // 2, r % 2].astype(F32), rows[r])
        source[...] = w if first else source[...] + w
        return w

    def products(w):
        rows = halves(w)

        @pl.loop(0, 8)
        def _(k):
            total = jnp.zeros((64, 128), F32)
            for r in range(16):
                total = total + times(bv[k, r // 2, r % 2].astype(F32), rows[r])
            pk[k] = total

    def message(step, way, target):
        return pltpu.make_async_remote_copy(
            src_ref=ax_out.at[step, way],
            dst_ref=ax_in.at[step, way],
            send_sem=asend.at[step, way],
            recv_sem=arecv.at[step, way],
            device_id=target,
            device_id_type=MESH,
        )

    products(weigh(field, True))

    for copy in ghosts:
        copy.wait_recv()
    lane8 = lax.broadcasted_iota(jnp.int32, (8, 128), 1)
    ghost_a = jnp.where((lane8 & 7) < 4, in_a[0], in_a[1])
    ghost_d[...] = jnp.where(ghost < 4, in_b[0, 4].astype(F32), in_b[1, 4].astype(F32))

    @pl.loop(0, 4)
    def _(pair):
        from_left = in_b[0, pair].astype(F32)
        from_right = in_b[1, pair].astype(F32)
        ghost_b[2 * pair] = jnp.where(ghost < 4, from_left, pltpu.roll(from_right, 4, 1))
        ghost_b[2 * pair + 1] = jnp.where(ghost < 4, pltpu.roll(from_left, 124, 1), from_right)

    for step in range(STEPS):
        if step > 0:
            a = -q[0:64]
            ghost_a = spread(-q[64:128])
            products(weigh(a, False))
        if step == STEPS - 1:
            pltpu.make_async_copy(source, source_out, store_sem.at[0]).start()

        ghost_w = jnp.dot(
            jnp.concatenate(split(times(ghost_d[...], ghost_a), 2), axis=1),
            same[0],
            preferred_element_type=F32,
        )
        rows = spread(ghost_w)
        moved = []
        for i, slots in enumerate(((0, 3, 5), (1, 6), (2, 4, 7))):
            p = jnp.concatenate([times(ghost_b[k], rows) for k in slots], axis=0)
            moved.append(
                jnp.dot(
                    jnp.concatenate(split(p, 2), axis=1), moves[i], preferred_element_type=F32
                )
            )
        from_ghosts = (
            moved[0][0:64] + moved[1][0:64] + moved[2][0:64],
            moved[0][64:128] + moved[2][64:128],
            moved[0][128:192] + moved[1][64:128] + moved[2][128:192],
        )

        def gathered(way, slot_left, slot_same, slot_right):
            to_left, to_right = pk[slot_left], pk[slot_right]
            main = jnp.where(lane == 127, 0.0, pltpu.roll(to_left, 127, 1))
            main = main + jnp.where(lane == 0, 0.0, pltpu.roll(to_right, 1, 1))
            if slot_same is not None:
                main = main + pk[slot_same]
            main = main + from_ghosts[way][:, :128]
            beyond = jnp.where(ghost == 3, to_left[:, 0:1], 0.0)
            beyond = jnp.where(ghost == 4, to_right[:, 127:128], beyond)
            beyond = beyond + from_ghosts[way][:, 128:]
            return main, beyond

        up = gathered(0, 0, 1, 2)
        up_s[0:64] = up[0]
        up_s[64:128] = up[1]
        down = gathered(2, 5, 6, 7)
        down_s[0:64] = down[0]
        down_s[64:128] = down[1]
        ax_out[step, 1] = up_s[pl.ds(0, 32, stride=4)]
        ax_out[step, 0] = down_s[pl.ds(3, 32, stride=4)]

        @pl.when(has_above)
        def _():
            message(step, 1, above).start()

        @pl.when(has_below)
        def _():
            message(step, 0, below).start()

        middle = gathered(1, 3, None, 4)
        for part in range(2):
            lifted = pltpu.roll(up[part].reshape(8, 8, 128), 7, 1).reshape(64, 128)
            dropped = pltpu.roll(down[part].reshape(8, 8, 128), 1, 1).reshape(64, 128)
            q[64 * part : 64 * part + 64] = (
                middle[part]
                + jnp.where((sub & 3) == 3, 0.0, lifted)
                + jnp.where((sub & 3) == 0, 0.0, dropped)
            )

        @pl.when(has_above)
        def _():
            message(step, 0, above).wait_recv()

        @pl.when(has_below)
        def _():
            message(step, 1, below).wait_recv()

        q[pl.ds(0, 32, stride=4)] = q[pl.ds(0, 32, stride=4)] + ax_in[step, 0]
        q[pl.ds(3, 32, stride=4)] = q[pl.ds(3, 32, stride=4)] + ax_in[step, 1]

    av[...] = -q[0:64]
    last = pltpu.make_async_copy(av, initial_out, store_sem.at[1])
    last.start()
    for copy in ghosts:
        copy.wait_send()
    for step in range(STEPS):

        @pl.when(has_above)
        def _():
            message(step, 1, above).wait_send()

        @pl.when(has_below)
        def _():
            message(step, 0, below).wait_send()

    pltpu.make_async_copy(source, source_out, store_sem.at[0]).wait()
    last.wait()


def per_device(cotangent, off_blocks, diag_inverse):
    vmem, dma = pltpu.VMEM, pltpu.SemaphoreType.DMA
    anywhere = pl.BlockSpec(memory_space=pl.ANY)
    hbm = pl.BlockSpec(memory_space=pltpu.HBM)
    source, initial = pl.pallas_call(
        kernel,
        out_shape=[jax.ShapeDtypeStruct((64, 128), F32)] * 2,
        in_specs=[hbm] * 3,
        out_specs=[anywhere] * 2,
        scratch_shapes=[
            vmem((64, 128), F32),
            vmem((8, 8, 2, 64, 128), BF16),
            vmem((8, 2, 64, 128), BF16),
            vmem((64, 128), F32),
            vmem((8, 64, 128), F32),
            vmem((64, 128), F32),
            vmem((2, 5, 64, 128), BF16),
            vmem((2, 5, 64, 128), BF16),
            vmem((8, 128), F32),
            vmem((2, 8, 128), F32),
            vmem((8, 64, 128), F32),
            vmem((128, 128), F32),
            vmem((128, 128), F32),
            vmem((128, 128), F32),
            vmem((STEPS, 2, 32, 128), F32),
            vmem((STEPS, 2, 32, 128), F32),
            vmem((256, 128), BF16),
            vmem((2, 256, 128), BF16),
            vmem((3, 256, 256), BF16),
            dma((10,)),
            dma((2,)),
            dma((4,)),
            dma((4,)),
            dma((STEPS, 2)),
            dma((STEPS, 2)),
        ],
        compiler_params=pltpu.CompilerParams(
            collective_id=0, has_side_effects=True, vmem_limit_bytes=60 << 20
        ),
        cost_estimate=pl.CostEstimate(
            flops=10 << 20, bytes_accessed=5 << 19, transcendentals=0
        ),
    )(
        cotangent.reshape(64, 128),
        off_blocks.reshape(8, 8, 2, 64, 128),
        diag_inverse.reshape(8, 2, 64, 128),
    )
    return source.reshape(cotangent.shape), initial.reshape(cotangent.shape)


def solution(mesh):
    return jax.shard_map(
        per_device,
        mesh=mesh,
        in_specs=(
            P(None, "ax", "circ"),
            P(None, None, None, "ax", "circ"),
            P(None, None, "ax", "circ"),
        ),
        out_specs=(P(None, "ax", "circ"), P(None, "ax", "circ")),
        check_vma=False,
    )
```

```python
import functools

import jax
import jax.numpy as jnp
from jax import lax
from jax.experimental import pallas as pl
from jax.experimental.pallas import tpu as pltpu
from jax.sharding import PartitionSpec as P

STEPS = 4
MESH = pl.DeviceIdType.MESH
F32 = jnp.float32
BF16 = jnp.bfloat16


def halves(field):
    sub = lax.broadcasted_iota(jnp.int32, (8, 128), 0)
    out = []
    for v in range(8):
        here = field[8 * v : 8 * v + 8]
        turned = pltpu.roll(here, 4, 0)
        out.append(jnp.where(sub < 4, here, turned))
        out.append(jnp.where(sub < 4, turned, here))
    return out


def spread(field):
    sub = lax.broadcasted_iota(jnp.int32, (8, 128), 0)
    group = lax.broadcasted_iota(jnp.int32, (8, 128), 1) >> 3
    total = jnp.zeros((8, 128), F32)
    for v in range(8):
        total = jnp.where(group == 2 * v + (sub >> 2), field[8 * v : 8 * v + 8], total)
    return total + pltpu.roll(total, 4, 0)


def split(x, parts):
    out = []
    for _ in range(parts):
        part = x.astype(BF16)
        out.append(part)
        x = x - part.astype(F32)
    return out


def times(blocks, rows):
    return (blocks.reshape(8, 8, 128) * rows[None]).reshape(64, 128)


def kernel(
    cot,
    off,
    diag,
    source_out,
    initial_out,
    av,
    bv,
    dv,
    source,
    edge_b,
    ghost_b,
    ghost_a,
    out_b,
    out_a,
    edge_w,
    strip_b,
    strip_d,
    pk,
    up_s,
    down_s,
    q,
    ax_out,
    ax_in,
    pick,
    same,
    moves,
    load_sem,
    store_sem,
    gsend,
    grecv,
    asend,
    arecv,
):
    ax, circ = lax.axis_index("ax"), lax.axis_index("circ")
    n_ax, n_circ = lax.axis_size("ax"), lax.axis_size("circ")
    right = (ax, lax.rem(circ + 1, n_circ))
    left = (ax, lax.rem(circ + n_circ - 1, n_circ))
    above, below = (ax - 1, circ), (ax + 1, circ)
    has_above, has_below = ax > 0, ax < n_ax - 1

    loads = [
        pltpu.make_async_copy(cot, av, load_sem.at[8]),
        pltpu.make_async_copy(diag, dv, load_sem.at[9]),
    ]
    for copy in loads:
        copy.start()

    def load(k):
        return pltpu.make_async_copy(off.at[k], bv.at[k], load_sem.at[k])

    for k in range(8):
        load(k).start()

    barrier = pltpu.get_barrier_semaphore()

    for way, there in ((0, has_above), (1, has_below)):

        @pl.when(jnp.logical_not(there))
        def _(way=way):
            ax_in[:, way] = jnp.zeros((STEPS, 16, 128), F32)
            edge_b[2 * way] = jnp.zeros((9, 64, 128), BF16)
            ghost_b[2 * way] = jnp.zeros((2, 5, 64, 128), BF16)
            ghost_a[2 * way] = jnp.zeros((2, 8, 128), F32)
            edge_w[2 * way] = jnp.zeros((STEPS - 1, 8, 128), F32)

    pl.semaphore_signal(barrier, inc=1, device_id=left, device_id_type=MESH)

    @pl.when(has_above)
    def _():
        pl.semaphore_signal(barrier, inc=1, device_id=above, device_id_type=MESH)

    @pl.when(has_below)
    def _():
        pl.semaphore_signal(barrier, inc=1, device_id=below, device_id_type=MESH)

    row = lax.broadcasted_iota(jnp.int32, (256, 128), 0)
    col = lax.broadcasted_iota(jnp.int32, (256, 128), 1)
    at_edge = ((row + 4) & 127) == (col & 7)
    pick[...] = jnp.where(at_edge & (((col >> 3) & 1) == (row >> 7)), 1.0, 0.0).astype(BF16)
    same[0] = jnp.where((row & 7) == (col & 7), 1.0, 0.0).astype(BF16)
    same[1] = jnp.where(at_edge, 1.0, 0.0).astype(BF16)
    for i, shift in enumerate((-1, 0, 1)):
        moves[i] = jnp.where((col & 7) == (row & 7) + shift, 1.0, 0.0).astype(BF16)

    lane = lax.broadcasted_iota(jnp.int32, (64, 128), 1)
    sub = lax.broadcasted_iota(jnp.int32, (64, 128), 0)
    lane8 = lax.broadcasted_iota(jnp.int32, (8, 128), 1)
    low, low8 = (lane & 7) < 4, (lane8 & 7) < 4

    def pick_edges(blocks):
        both = jnp.concatenate(
            [blocks[:, 0].reshape(512, 128), blocks[:, 1].reshape(512, 128)], axis=1
        )
        found = jnp.dot(both, pick[...], preferred_element_type=F32)
        total = found[0:64]
        for p in range(1, 8):
            total = jnp.where((lane >> 4) == p, found[64 * p : 64 * p + 64], total)
        return total

    def edges_of(field, parts):
        total = jnp.zeros((64, 128), F32)
        for part in split(field, parts):
            total = total + jnp.dot(part, same[1, :128], preferred_element_type=F32)
        return spread(total)

    loads[0].wait()
    field = av[...]
    out_a[...] = edges_of(field, 3)
    loads[1].wait()
    edges = pick_edges(dv[...]).astype(BF16)
    edge_b[1, 8] = edges
    out_b[0, 4] = edges
    out_b[1, 4] = edges
    for half in range(2):
        for k in range(4 * half, 4 * half + 4):
            load(k).wait()
        for pair in (2 * half, 2 * half + 1):
            first = pick_edges(bv[2 * pair])
            second = pick_edges(bv[2 * pair + 1])
            edge_b[1, 2 * pair] = first.astype(BF16)
            edge_b[1, 2 * pair + 1] = second.astype(BF16)
            out_b[0, pair] = jnp.where(low, first, pltpu.roll(second, 4, 1)).astype(BF16)
            out_b[1, pair] = jnp.where(low, pltpu.roll(first, 124, 1), second).astype(BF16)

    pl.semaphore_wait(
        barrier, 1 + has_above.astype(jnp.int32) + has_below.astype(jnp.int32)
    )

    ghosts = []
    for side, target in ((0, right), (1, left)):
        for part, (src, dst) in enumerate(
            ((out_b.at[side], ghost_b.at[1, side]), (out_a, ghost_a.at[1, side]))
        ):
            ghosts.append(
                pltpu.make_async_remote_copy(
                    src_ref=src,
                    dst_ref=dst,
                    send_sem=gsend.at[2 * side + part],
                    recv_sem=grecv.at[2 * side + part],
                    device_id=target,
                    device_id_type=MESH,
                )
            )
    ghosts[0].start()
    ghosts[1].start()

    def along(src, dst, slot, way):
        return pltpu.make_async_remote_copy(
            src_ref=src,
            dst_ref=dst,
            send_sem=asend.at[slot, way],
            recv_sem=arecv.at[slot, way],
            device_id=below if way == 0 else above,
            device_id_type=MESH,
        )

    def rows_copy(step, way):
        return along(ax_out.at[step, way], ax_in.at[step, way], step, way)

    def blocks_copy(way):
        return along(edge_b.at[1], edge_b.at[2 * way], STEPS, way)

    def weighted_copy(way):
        return along(edge_w.at[1], edge_w.at[2 * way], STEPS + 1, way)

    def forward_copies(side, way):
        slot = STEPS + 2 + 2 * side
        return (
            along(ghost_b.at[1, side], ghost_b.at[2 * way, side], slot, way),
            along(ghost_a.at[1, side], ghost_a.at[2 * way, side], slot + 1, way),
        )

    def start(copies):
        for way, there in ((0, has_below), (1, has_above)):

            @pl.when(there)
            def _(way=way):
                for copy in copies(way):
                    copy.start()

    def arrive(copies):
        for way, there in ((0, has_above), (1, has_below)):

            @pl.when(there)
            def _(way=way):
                for copy in copies(way):
                    copy.wait_recv()

    def sent(copies):
        for way, there in ((0, has_below), (1, has_above)):

            @pl.when(there)
            def _(way=way):
                for copy in copies(way):
                    copy.wait_send()

    for step in range(STEPS):
        rows = halves(field)
        w = jnp.zeros((64, 128), F32)
        for r in range(16):
            w = w + times(dv[r // 2, r % 2].astype(F32), rows[r])
        source[...] = w if step == 0 else source[...] + w
        rows = halves(w)

        @pl.loop(0, 8)
        def _(k):
            total = jnp.zeros((64, 128), F32)
            for r in range(16):
                total = total + times(bv[k, r // 2, r % 2].astype(F32), rows[r])
            pk[k] = total

        def gathered(slot_left, slot_same, slot_right):
            main = jnp.where(lane == 127, 0.0, pltpu.roll(pk[slot_left], 127, 1))
            main = main + jnp.where(lane == 0, 0.0, pltpu.roll(pk[slot_right], 1, 1))
            return main if slot_same is None else main + pk[slot_same]

        up = gathered(0, 1, 2)
        down = gathered(5, 6, 7)
        up_s[...] = up
        down_s[...] = down
        ax_out[step, 1] = up_s[pl.ds(0, 16, stride=4)]
        ax_out[step, 0] = down_s[pl.ds(3, 16, stride=4)]
        start(lambda way, step=step: [rows_copy(step, way)])
        if step == 0:
            start(lambda way: [blocks_copy(way)])
        if step < STEPS - 1:
            edge_w[1, step] = edges_of(w, 2)
        if step == STEPS - 2:
            start(lambda way: [weighted_copy(way)])
        lifted = pltpu.roll(up.reshape(8, 8, 128), 7, 1).reshape(64, 128)
        dropped = pltpu.roll(down.reshape(8, 8, 128), 1, 1).reshape(64, 128)
        q[...] = (
            gathered(3, None, 4)
            + jnp.where((sub & 3) == 3, 0.0, lifted)
            + jnp.where((sub & 3) == 0, 0.0, dropped)
        )
        if step >= STEPS - 2:
            side = step - (STEPS - 2)
            ghosts[2 * side].wait_recv()
            ghosts[2 * side + 1].wait_recv()
            if side == 0:
                ghosts[2].start()
                ghosts[3].start()
            start(lambda way, side=side: forward_copies(side, way))
        arrive(lambda way, step=step: [rows_copy(step, way)])
        q[pl.ds(0, 16, stride=4)] = q[pl.ds(0, 16, stride=4)] + ax_in[step, 0]
        q[pl.ds(3, 16, stride=4)] = q[pl.ds(3, 16, stride=4)] + ax_in[step, 1]
        field = -q[...]
    av[...] = field

    def assemble(side, block):
        for pair in range(4):
            ghost = ghost_b[block, side, pair].astype(F32)
            first = edge_b[block, 2 * pair].astype(F32)
            second = edge_b[block, 2 * pair + 1].astype(F32)
            if side == 0:
                strip_b[side, block, 2 * pair] = jnp.where(low, ghost, first)
                strip_b[side, block, 2 * pair + 1] = jnp.where(
                    low, pltpu.roll(ghost, 124, 1), second
                )
            else:
                strip_b[side, block, 2 * pair] = jnp.where(low, first, pltpu.roll(ghost, 4, 1))
                strip_b[side, block, 2 * pair + 1] = jnp.where(low, second, ghost)
        ghost = ghost_b[block, side, 4].astype(F32)
        mine = edge_b[block, 8].astype(F32)
        strip_d[side, block] = (
            jnp.where(low, ghost, mine) if side == 0 else jnp.where(low, mine, ghost)
        )

    def strip(side):
        arrive(lambda way: forward_copies(side, way))
        for block in range(3):
            assemble(side, block)
        blocks = range(3)
        outward = (0, 3, 5) if side == 0 else (2, 4, 7)
        crossing = (lane8 & 7) == (4 if side == 0 else 3)
        d, added = None, None
        for step in range(STEPS):
            if step == 0:
                fields = [ghost_a[block, side] for block in blocks]
                if side == 0:
                    fields = [jnp.where(low8, a, 0.0) for a in fields]
                else:
                    fields = [jnp.where(low8, 0.0, a) for a in fields]
            else:
                fields = [spread(x) for x in d]
            p = [times(strip_d[side, block], fields[block]) for block in blocks]
            w = jnp.dot(
                jnp.concatenate(split(jnp.concatenate(p, axis=0), 2), axis=1),
                same[0],
                preferred_element_type=F32,
            )
            added = w[64:128] if step == 0 else added + w[64:128]
            rows = [spread(w[64 * block : 64 * block + 64]) for block in blocks]
            rows_out = rows
            if step < STEPS - 1:
                rows_out = [
                    rows[block] + jnp.where(crossing, edge_w[block, step], 0.0)
                    for block in blocks
                ]

            def flow(k, block):
                return times(
                    strip_b[side, block, k], (rows_out if k in outward else rows)[block]
                )

            def turned(x, by):
                return pltpu.roll(x.reshape(8, 8, 128), by, 1).reshape(64, 128)

            targets = blocks if step < STEPS - 1 else (1,)
            moved = jnp.zeros((64 * len(targets), 128), F32)
            for i, (k_up, k_level, k_down) in enumerate(((0, 3, 5), (1, None, 6), (2, 4, 7))):
                ups = {block: flow(k_up, block) for block in blocks}
                downs = {block: flow(k_down, block) for block in blocks}
                sums = []
                for block in targets:
                    total = turned(ups[block], 7)
                    over = turned(ups[block + 1], 3) if block < 2 else 0.0
                    total = jnp.where((sub & 3) == 3, over, total)
                    falling = turned(downs[block], 1)
                    over = turned(downs[block - 1], 5) if block > 0 else 0.0
                    total = total + jnp.where((sub & 3) == 0, over, falling)
                    if k_level is not None:
                        total = total + flow(k_level, block)
                    sums.append(total)
                moved = moved + jnp.dot(
                    jnp.concatenate(split(jnp.concatenate(sums, axis=0), 2), axis=1),
                    moves[i],
                    preferred_element_type=F32,
                )
            d = [-moved[64 * n : 64 * n + 64] for n in range(len(targets))]
        return added, d[0]

    arrive(lambda way: [blocks_copy(way)])
    arrive(lambda way: [weighted_copy(way)])
    added_right, d_right = strip(1)
    added_left, d_left = strip(0)

    def with_strips(u, left_strip, right_strip):
        u = u + jnp.where(lane < 4, pltpu.roll(left_strip, 124, 1), 0.0)
        return u + jnp.where(lane >= 124, pltpu.roll(right_strip, 4, 1), 0.0)

    source[...] = with_strips(source[...], added_left, added_right)
    av[...] = with_strips(av[...], d_left, d_right)
    stores = [
        pltpu.make_async_copy(source, source_out, store_sem.at[0]),
        pltpu.make_async_copy(av, initial_out, store_sem.at[1]),
    ]
    for copy in stores:
        copy.start()
    for copy in ghosts:
        copy.wait_send()
    for step in range(STEPS):
        sent(lambda way, step=step: [rows_copy(step, way)])
    sent(lambda way: [blocks_copy(way), weighted_copy(way)])
    for side in range(2):
        sent(lambda way, side=side: forward_copies(side, way))
    for copy in stores:
        copy.wait()


def per_device(cotangent, off_blocks, diag_inverse):
    vmem, dma = pltpu.VMEM, pltpu.SemaphoreType.DMA
    anywhere = pl.BlockSpec(memory_space=pl.ANY)
    hbm = pl.BlockSpec(memory_space=pltpu.HBM)
    source, initial = pl.pallas_call(
        kernel,
        out_shape=[jax.ShapeDtypeStruct((64, 128), F32)] * 2,
        in_specs=[hbm] * 3,
        out_specs=[anywhere] * 2,
        scratch_shapes=[
            vmem((64, 128), F32),
            vmem((8, 8, 2, 64, 128), BF16),
            vmem((8, 2, 64, 128), BF16),
            vmem((64, 128), F32),
            vmem((3, 9, 64, 128), BF16),
            vmem((3, 2, 5, 64, 128), BF16),
            vmem((3, 2, 8, 128), F32),
            vmem((2, 5, 64, 128), BF16),
            vmem((8, 128), F32),
            vmem((3, STEPS - 1, 8, 128), F32),
            vmem((2, 3, 8, 64, 128), F32),
            vmem((2, 3, 64, 128), F32),
            vmem((8, 64, 128), F32),
            vmem((64, 128), F32),
            vmem((64, 128), F32),
            vmem((64, 128), F32),
            vmem((STEPS, 2, 16, 128), F32),
            vmem((STEPS, 2, 16, 128), F32),
            vmem((256, 128), BF16),
            vmem((2, 256, 128), BF16),
            vmem((3, 256, 128), BF16),
            dma((10,)),
            dma((2,)),
            dma((4,)),
            dma((4,)),
            dma((STEPS + 6, 2)),
            dma((STEPS + 6, 2)),
        ],
        compiler_params=pltpu.CompilerParams(
            collective_id=0, has_side_effects=True, vmem_limit_bytes=60 << 20
        ),
        cost_estimate=pl.CostEstimate(
            flops=10 << 20, bytes_accessed=5 << 19, transcendentals=0
        ),
    )(
        cotangent.reshape(64, 128),
        off_blocks.reshape(8, 8, 2, 64, 128),
        diag_inverse.reshape(8, 2, 64, 128),
    )
    return source.reshape(cotangent.shape), initial.reshape(cotangent.shape)


def solution(mesh):
    return jax.shard_map(
        per_device,
        mesh=mesh,
        in_specs=(
            P(None, "ax", "circ"),
            P(None, None, None, "ax", "circ"),
            P(None, None, "ax", "circ"),
        ),
        out_specs=(P(None, "ax", "circ"), P(None, "ax", "circ")),
        check_vma=False,
    )
```

```python
import functools

import jax
import jax.numpy as jnp
from jax import lax
from jax.experimental import pallas as pl
from jax.experimental.pallas import tpu as pltpu
from jax.sharding import PartitionSpec as P

STEPS = 4
MESH = pl.DeviceIdType.MESH
F32 = jnp.float32
BF16 = jnp.bfloat16

SLOTS = (((2, 4, 7), (1, 6), (0, 3, 5)), ((0, 3, 5), (1, 6), (2, 4, 7)))


def halves(field):
    sub = lax.broadcasted_iota(jnp.int32, (8, 128), 0)
    out = []
    for v in range(8):
        here = field[8 * v : 8 * v + 8]
        turned = pltpu.roll(here, 4, 0)
        out.append(jnp.where(sub < 4, here, turned))
        out.append(jnp.where(sub < 4, turned, here))
    return out


def spread(field):
    sub = lax.broadcasted_iota(jnp.int32, (8, 128), 0)
    group = lax.broadcasted_iota(jnp.int32, (8, 128), 1) >> 3
    total = jnp.zeros((8, 128), F32)
    for v in range(8):
        total = jnp.where(group == 2 * v + (sub >> 2), field[8 * v : 8 * v + 8], total)
    return total + pltpu.roll(total, 4, 0)


def split(x, parts):
    out = []
    for _ in range(parts):
        part = x.astype(BF16)
        out.append(part)
        x = x - part.astype(F32)
    return out


def times(blocks, rows):
    return (blocks.reshape(8, 8, 128) * rows[None]).reshape(64, 128)


def kernel(
    cot,
    off,
    diag,
    source_out,
    initial_out,
    av,
    bv,
    dv,
    source,
    edge_b,
    ghost_b,
    ghost_a,
    out_b,
    out_a,
    edge_w,
    strip_b,
    strip_d,
    pk,
    up_s,
    down_s,
    q,
    ax_out,
    ax_in,
    pick_s,
    same,
    moves,
    load_sem,
    store_sem,
    gsend,
    grecv,
    asend,
    arecv,
):
    ax, circ = lax.axis_index("ax"), lax.axis_index("circ")
    n_ax, n_circ = lax.axis_size("ax"), lax.axis_size("circ")
    right = (ax, lax.rem(circ + 1, n_circ))
    left = (ax, lax.rem(circ + n_circ - 1, n_circ))
    above, below = (ax - 1, circ), (ax + 1, circ)
    has_above, has_below = ax > 0, ax < n_ax - 1

    loads = [
        pltpu.make_async_copy(cot, av, load_sem.at[8]),
        pltpu.make_async_copy(diag, dv, load_sem.at[9]),
    ]
    for copy in loads:
        copy.start()

    def load(k):
        return pltpu.make_async_copy(off.at[k], bv.at[k], load_sem.at[k])

    for group in SLOTS[0]:
        for k in group:
            load(k).start()

    barrier = pltpu.get_barrier_semaphore()

    for way, there in ((0, has_above), (1, has_below)):

        @pl.when(jnp.logical_not(there))
        def _(way=way):
            ax_in[:, way] = jnp.zeros((STEPS, 16, 128), F32)
            edge_b[2 * way] = jnp.zeros((9, 64, 128), BF16)
            ghost_b[2 * way] = jnp.zeros((2, 4, 64, 128), BF16)
            ghost_a[2 * way] = jnp.zeros((2, 8, 128), F32)
            edge_w[2 * way] = jnp.zeros((STEPS - 1, 8, 128), F32)

    pl.semaphore_signal(barrier, inc=1, device_id=left, device_id_type=MESH)

    @pl.when(has_above)
    def _():
        pl.semaphore_signal(barrier, inc=1, device_id=above, device_id_type=MESH)

    @pl.when(has_below)
    def _():
        pl.semaphore_signal(barrier, inc=1, device_id=below, device_id_type=MESH)

    row = lax.broadcasted_iota(jnp.int32, (256, 128), 0)
    col = lax.broadcasted_iota(jnp.int32, (256, 128), 1)
    at_edge = ((row + 4) & 127) == (col & 7)
    pick_s[...] = jnp.where(at_edge & (((col >> 3) & 1) == (row >> 7)), 1.0, 0.0).astype(BF16)
    same[0] = jnp.where((row & 7) == (col & 7), 1.0, 0.0).astype(BF16)
    same[1] = jnp.where(at_edge, 1.0, 0.0).astype(BF16)
    for i, shift in enumerate((-1, 0, 1)):
        moves[i] = jnp.where((col & 7) == (row & 7) + shift, 1.0, 0.0).astype(BF16)

    lane = lax.broadcasted_iota(jnp.int32, (64, 128), 1)
    sub = lax.broadcasted_iota(jnp.int32, (64, 128), 0)
    lane8 = lax.broadcasted_iota(jnp.int32, (8, 128), 1)
    low, low8 = (lane & 7) < 4, (lane8 & 7) < 4

    def pick_edges(blocks):
        both = jnp.concatenate(
            [blocks[:, 0].reshape(512, 128), blocks[:, 1].reshape(512, 128)], axis=1
        )
        found = jnp.dot(both, pick_s[...], preferred_element_type=F32)
        total = found[0:64]
        for p in range(1, 8):
            total = jnp.where((lane >> 4) == p, found[64 * p : 64 * p + 64], total)
        return total

    def edges_of(field, parts):
        total = jnp.zeros((64, 128), F32)
        for part in split(field, parts):
            total = total + jnp.dot(part, same[1, :128], preferred_element_type=F32)
        return spread(total)

    loads[0].wait()
    field = av[...]
    out_a[...] = edges_of(field, 3)
    loads[1].wait()
    picked = {8: pick_edges(dv[...])}

    def pick(slots):
        for k in slots:
            load(k).wait()
        for k in slots:
            picked[k] = pick_edges(bv[k])

    def pair(first, second):
        return jnp.where(low, picked[first], pltpu.roll(picked[second], 4, 1))

    def pair_high(first, second):
        return jnp.where(low, pltpu.roll(picked[first], 124, 1), picked[second])

    ghost = lane & 7

    def three(slots, at):
        total = jnp.where(ghost < 2, pltpu.roll(picked[slots[0]], (128 - at) % 128, 1), 0.0)
        for n in (1, 2):
            moved = pltpu.roll(picked[slots[n]], (128 + 2 * n - at) % 128, 1)
            total = jnp.where((ghost >> 1) == n, moved, total)
        return total

    towards, level, away = SLOTS[0]
    pick(towards)
    out_b[0, 0] = pair(towards[0], towards[1]).astype(BF16)
    out_b[0, 1] = pair(towards[2], 8).astype(BF16)
    pl.semaphore_wait(
        barrier, 1 + has_above.astype(jnp.int32) + has_below.astype(jnp.int32)
    )

    ghosts = []
    for side, target in ((0, right), (1, left)):
        for part, (src, dst) in enumerate(
            (
                (out_a, ghost_a.at[1, side]),
                (out_b.at[side, 0:2], ghost_b.at[1, side, 0:2]),
                (out_b.at[side, 2:4], ghost_b.at[1, side, 2:4]),
            )
        ):
            ghosts.append(
                pltpu.make_async_remote_copy(
                    src_ref=src,
                    dst_ref=dst,
                    send_sem=gsend.at[side, part],
                    recv_sem=grecv.at[side, part],
                    device_id=target,
                    device_id_type=MESH,
                )
            )
    ghosts[1].start()
    ghosts[0].start()
    pick(level + away)
    out_b[0, 2] = pair(*level).astype(BF16)
    out_b[0, 3] = three(away, 2).astype(BF16)
    ghosts[2].start()
    for k in range(9):
        edge_b[1, k] = picked[k].astype(BF16)
    towards, level, away = SLOTS[1]
    out_b[1, 0] = pair_high(towards[0], towards[1]).astype(BF16)
    out_b[1, 1] = pair_high(towards[2], 8).astype(BF16)
    out_b[1, 2] = pair_high(*level).astype(BF16)
    out_b[1, 3] = three(away, 4).astype(BF16)

    def along(src, dst, slot, way):
        return pltpu.make_async_remote_copy(
            src_ref=src,
            dst_ref=dst,
            send_sem=asend.at[slot, way],
            recv_sem=arecv.at[slot, way],
            device_id=below if way == 0 else above,
            device_id_type=MESH,
        )

    def rows_copy(step, way):
        return along(ax_out.at[step, way], ax_in.at[step, way], step, way)

    def blocks_copy(way):
        return along(edge_b.at[1], edge_b.at[2 * way], STEPS, way)

    def weighted_copy(way):
        return along(edge_w.at[1], edge_w.at[2 * way], STEPS + 1, way)

    def forward_copy(side, part, way):
        ref = (ghost_a, ghost_b, ghost_b)[part]
        at = ((), (slice(0, 2),), (slice(2, 4),))[part]
        return along(
            ref.at[(1, side) + at],
            ref.at[(2 * way, side) + at],
            STEPS + 2 + 3 * side + part,
            way,
        )

    def forward_copies(side, way):
        return [forward_copy(side, part, way) for part in range(3)]

    def start(copies):
        for way, there in ((0, has_below), (1, has_above)):

            @pl.when(there)
            def _(way=way):
                for copy in copies(way):
                    copy.start()

    def arrive(copies):
        for way, there in ((0, has_above), (1, has_below)):

            @pl.when(there)
            def _(way=way):
                for copy in copies(way):
                    copy.wait_recv()

    def sent(copies):
        for way, there in ((0, has_below), (1, has_above)):

            @pl.when(there)
            def _(way=way):
                for copy in copies(way):
                    copy.wait_send()

    def pass_on(side):
        for part in (1, 0, 2):
            ghosts[3 * side + part].wait_recv()
            if part != 1:
                parts = (0, 1) if part == 0 else (2,)
                start(lambda way: [forward_copy(side, n, way) for n in parts])
        if side == 0:
            for copy in ghosts[3:]:
                copy.start()

    for step in range(STEPS):
        rows = halves(field)
        w = jnp.zeros((64, 128), F32)
        for r in range(16):
            w = w + times(dv[r // 2, r % 2].astype(F32), rows[r])
        source[...] = w if step == 0 else source[...] + w
        rows = halves(w)

        @pl.loop(0, 8)
        def _(k):
            total = jnp.zeros((64, 128), F32)
            for r in range(16):
                total = total + times(bv[k, r // 2, r % 2].astype(F32), rows[r])
            pk[k] = total

        def gathered(slot_left, slot_same, slot_right):
            main = jnp.where(lane == 127, 0.0, pltpu.roll(pk[slot_left], 127, 1))
            main = main + jnp.where(lane == 0, 0.0, pltpu.roll(pk[slot_right], 1, 1))
            return main if slot_same is None else main + pk[slot_same]

        up = gathered(0, 1, 2)
        down = gathered(5, 6, 7)
        up_s[...] = up
        down_s[...] = down
        ax_out[step, 1] = up_s[pl.ds(0, 16, stride=4)]
        ax_out[step, 0] = down_s[pl.ds(3, 16, stride=4)]
        start(lambda way, step=step: [rows_copy(step, way)])
        if step == 0:
            start(lambda way: [blocks_copy(way)])
        if step < STEPS - 1:
            edge_w[1, step] = edges_of(w, 2)
        if step == STEPS - 2:
            start(lambda way: [weighted_copy(way)])
        lifted = pltpu.roll(up.reshape(8, 8, 128), 7, 1).reshape(64, 128)
        dropped = pltpu.roll(down.reshape(8, 8, 128), 1, 1).reshape(64, 128)
        q[...] = (
            gathered(3, None, 4)
            + jnp.where((sub & 3) == 3, 0.0, lifted)
            + jnp.where((sub & 3) == 0, 0.0, dropped)
        )
        if step == STEPS - 2:

            @pl.when(circ > 0)
            def _():
                pass_on(0)

        if step == STEPS - 1:
            pass_on(1)

            @pl.when(circ == 0)
            def _():
                pass_on(0)

        arrive(lambda way, step=step: [rows_copy(step, way)])
        q[pl.ds(0, 16, stride=4)] = q[pl.ds(0, 16, stride=4)] + ax_in[step, 0]
        q[pl.ds(3, 16, stride=4)] = q[pl.ds(3, 16, stride=4)] + ax_in[step, 1]
        field = -q[...]
    av[...] = field

    def assemble(side, block):
        towards, level, away = SLOTS[side]
        parts = [ghost_b[block, side, n].astype(F32) for n in range(4)]

        def put(to, k, part, by):
            found = pltpu.roll(parts[part], by % 128, 1) if by else parts[part]
            mine = edge_b[block, k].astype(F32)
            to[...] = jnp.where(low if side == 0 else ~low, found, mine)

        base = 4 * side
        for n, k in enumerate(towards):
            put(strip_b.at[side, block, k], k, n // 2, base - 4 * (n % 2))
        put(strip_d.at[side, block], 8, 1, base - 4)
        for n, k in enumerate(level):
            put(strip_b.at[side, block, k], k, 2, base - 4 * n)
        for n, k in enumerate(away):
            put(strip_b.at[side, block, k], k, 3, (2 if side == 0 else 4) - 2 * n)

    def strip(side):
        assemble(side, 1)
        arrive(lambda way: forward_copies(side, way))
        assemble(side, 0)
        assemble(side, 2)
        blocks = range(3)
        outward = (0, 3, 5) if side == 0 else (2, 4, 7)
        crossing = (lane8 & 7) == (4 if side == 0 else 3)
        d, added = None, None
        for step in range(STEPS):
            if step == 0:
                fields = [ghost_a[block, side] for block in blocks]
                if side == 0:
                    fields = [jnp.where(low8, a, 0.0) for a in fields]
                else:
                    fields = [jnp.where(low8, 0.0, a) for a in fields]
            else:
                fields = [spread(x) for x in d]
            p = [times(strip_d[side, block], fields[block]) for block in blocks]
            w = jnp.dot(
                jnp.concatenate(split(jnp.concatenate(p, axis=0), 2), axis=1),
                same[0],
                preferred_element_type=F32,
            )
            added = w[64:128] if step == 0 else added + w[64:128]
            rows = [spread(w[64 * block : 64 * block + 64]) for block in blocks]
            rows_out = rows
            if step < STEPS - 1:
                rows_out = [
                    rows[block] + jnp.where(crossing, edge_w[block, step], 0.0)
                    for block in blocks
                ]

            def flow(k, block):
                return times(
                    strip_b[side, block, k], (rows_out if k in outward else rows)[block]
                )

            def turned(x, by):
                return pltpu.roll(x.reshape(8, 8, 128), by, 1).reshape(64, 128)

            targets = blocks if step < STEPS - 1 else (1,)
            moved = jnp.zeros((64 * len(targets), 128), F32)
            for i, (k_up, k_level, k_down) in enumerate(((0, 3, 5), (1, None, 6), (2, 4, 7))):
                ups = {block: flow(k_up, block) for block in blocks}
                downs = {block: flow(k_down, block) for block in blocks}
                sums = []
                for block in targets:
                    total = turned(ups[block], 7)
                    over = turned(ups[block + 1], 3) if block < 2 else 0.0
                    total = jnp.where((sub & 3) == 3, over, total)
                    falling = turned(downs[block], 1)
                    over = turned(downs[block - 1], 5) if block > 0 else 0.0
                    total = total + jnp.where((sub & 3) == 0, over, falling)
                    if k_level is not None:
                        total = total + flow(k_level, block)
                    sums.append(total)
                moved = moved + jnp.dot(
                    jnp.concatenate(split(jnp.concatenate(sums, axis=0), 2), axis=1),
                    moves[i],
                    preferred_element_type=F32,
                )
            d = [-moved[64 * n : 64 * n + 64] for n in range(len(targets))]
        return added, d[0]

    arrive(lambda way: [blocks_copy(way)])
    arrive(lambda way: [weighted_copy(way)])
    added_right, d_right = strip(1)
    added_left, d_left = strip(0)

    def with_strips(u, left_strip, right_strip):
        u = u + jnp.where(lane < 4, pltpu.roll(left_strip, 124, 1), 0.0)
        return u + jnp.where(lane >= 124, pltpu.roll(right_strip, 4, 1), 0.0)

    source[...] = with_strips(source[...], added_left, added_right)
    av[...] = with_strips(av[...], d_left, d_right)
    stores = [
        pltpu.make_async_copy(source, source_out, store_sem.at[0]),
        pltpu.make_async_copy(av, initial_out, store_sem.at[1]),
    ]
    for copy in stores:
        copy.start()
    for copy in ghosts:
        copy.wait_send()
    for step in range(STEPS):
        sent(lambda way, step=step: [rows_copy(step, way)])
    sent(lambda way: [blocks_copy(way), weighted_copy(way)])
    for side in range(2):
        sent(lambda way, side=side: forward_copies(side, way))
    for copy in stores:
        copy.wait()


def written(source, initial, source_out, initial_out):
    source_out[...] = source[...]
    initial_out[...] = initial[...]


def per_device(cotangent, off_blocks, diag_inverse):
    vmem, dma = pltpu.VMEM, pltpu.SemaphoreType.DMA
    anywhere = pl.BlockSpec(memory_space=pl.ANY)
    hbm = pl.BlockSpec(memory_space=pltpu.HBM)
    source, initial = pl.pallas_call(
        kernel,
        out_shape=[jax.ShapeDtypeStruct((64, 128), F32)] * 2,
        in_specs=[hbm] * 3,
        out_specs=[anywhere] * 2,
        scratch_shapes=[
            vmem((64, 128), F32),
            vmem((8, 8, 2, 64, 128), BF16),
            vmem((8, 2, 64, 128), BF16),
            vmem((64, 128), F32),
            vmem((3, 9, 64, 128), BF16),
            vmem((3, 2, 4, 64, 128), BF16),
            vmem((3, 2, 8, 128), F32),
            vmem((2, 4, 64, 128), BF16),
            vmem((8, 128), F32),
            vmem((3, STEPS - 1, 8, 128), F32),
            vmem((2, 3, 8, 64, 128), F32),
            vmem((2, 3, 64, 128), F32),
            vmem((8, 64, 128), F32),
            vmem((64, 128), F32),
            vmem((64, 128), F32),
            vmem((64, 128), F32),
            vmem((STEPS, 2, 16, 128), F32),
            vmem((STEPS, 2, 16, 128), F32),
            vmem((256, 128), BF16),
            vmem((2, 256, 128), BF16),
            vmem((3, 256, 128), BF16),
            dma((10,)),
            dma((2,)),
            dma((2, 3)),
            dma((2, 3)),
            dma((STEPS + 8, 2)),
            dma((STEPS + 8, 2)),
        ],
        compiler_params=pltpu.CompilerParams(
            collective_id=0, has_side_effects=True, vmem_limit_bytes=60 << 20
        ),
        cost_estimate=pl.CostEstimate(
            flops=10 << 20, bytes_accessed=5 << 19, transcendentals=0
        ),
    )(
        cotangent.reshape(64, 128),
        off_blocks.reshape(8, 8, 2, 64, 128),
        diag_inverse.reshape(8, 2, 64, 128),
    )
    source, initial = pl.pallas_call(
        written,
        out_shape=[jax.ShapeDtypeStruct((64, 128), F32)] * 2,
        in_specs=[pl.BlockSpec(memory_space=vmem)] * 2,
        out_specs=[pl.BlockSpec(memory_space=vmem)] * 2,
    )(source, initial)
    return source.reshape(cotangent.shape), initial.reshape(cotangent.shape)


def solution(mesh):
    return jax.shard_map(
        per_device,
        mesh=mesh,
        in_specs=(
            P(None, "ax", "circ"),
            P(None, None, None, "ax", "circ"),
            P(None, None, "ax", "circ"),
        ),
        out_specs=(P(None, "ax", "circ"), P(None, "ax", "circ")),
        check_vma=False,
    )
```

```python
import functools

import jax
import jax.numpy as jnp
from jax import lax
from jax.experimental import pallas as pl
from jax.experimental.pallas import tpu as pltpu
from jax.sharding import PartitionSpec as P

STEPS = 4
MESH = pl.DeviceIdType.MESH
F32 = jnp.float32
BF16 = jnp.bfloat16

SLOTS = (((2, 4, 7), (1, 6), (0, 3, 5)), ((0, 3, 5), (1, 6), (2, 4, 7)))


def halves(field):
    sub = lax.broadcasted_iota(jnp.int32, (8, 128), 0)
    out = []
    for v in range(8):
        here = field[8 * v : 8 * v + 8]
        turned = pltpu.roll(here, 4, 0)
        out.append(jnp.where(sub < 4, here, turned))
        out.append(jnp.where(sub < 4, turned, here))
    return out


def spread(field):
    sub = lax.broadcasted_iota(jnp.int32, (8, 128), 0)
    group = lax.broadcasted_iota(jnp.int32, (8, 128), 1) >> 3
    total = jnp.zeros((8, 128), F32)
    for v in range(8):
        total = jnp.where(group == 2 * v + (sub >> 2), field[8 * v : 8 * v + 8], total)
    return total + pltpu.roll(total, 4, 0)


def split(x, parts):
    out = []
    for _ in range(parts):
        part = x.astype(BF16)
        out.append(part)
        x = x - part.astype(F32)
    return out


def times(blocks, rows):
    return (blocks.reshape(8, 8, 128) * rows[None]).reshape(64, 128)


def kernel(
    cot,
    off,
    diag,
    source_out,
    initial_out,
    av,
    bv,
    dv,
    source,
    edge_b,
    ghost_b,
    ghost_a,
    out_b,
    out_a,
    edge_w,
    strip_b,
    strip_d,
    pk,
    up_s,
    down_s,
    q,
    ax_out,
    ax_in,
    pick_s,
    same,
    moves,
    load_sem,
    gsend,
    grecv,
    asend,
    arecv,
):
    ax, circ = lax.axis_index("ax"), lax.axis_index("circ")
    n_ax, n_circ = lax.axis_size("ax"), lax.axis_size("circ")
    right = (ax, lax.rem(circ + 1, n_circ))
    left = (ax, lax.rem(circ + n_circ - 1, n_circ))
    above, below = (ax - 1, circ), (ax + 1, circ)
    has_above, has_below = ax > 0, ax < n_ax - 1

    loads = [
        pltpu.make_async_copy(cot, av, load_sem.at[8]),
        pltpu.make_async_copy(diag, dv, load_sem.at[9]),
    ]
    for copy in loads:
        copy.start()

    def load(k):
        return pltpu.make_async_copy(off.at[k], bv.at[k], load_sem.at[k])

    for group in SLOTS[0]:
        for k in group:
            load(k).start()

    barrier = pltpu.get_barrier_semaphore()

    for way, there in ((0, has_above), (1, has_below)):

        @pl.when(jnp.logical_not(there))
        def _(way=way):
            ax_in[:, way] = jnp.zeros((STEPS, 16, 128), F32)
            edge_b[2 * way] = jnp.zeros((9, 64, 128), BF16)
            ghost_b[2 * way] = jnp.zeros((2, 4, 64, 128), BF16)
            ghost_a[2 * way] = jnp.zeros((2, 8, 128), F32)
            edge_w[2 * way] = jnp.zeros((STEPS - 1, 8, 128), F32)

    pl.semaphore_signal(barrier, inc=1, device_id=left, device_id_type=MESH)

    @pl.when(has_above)
    def _():
        pl.semaphore_signal(barrier, inc=1, device_id=above, device_id_type=MESH)

    @pl.when(has_below)
    def _():
        pl.semaphore_signal(barrier, inc=1, device_id=below, device_id_type=MESH)

    row = lax.broadcasted_iota(jnp.int32, (256, 128), 0)
    col = lax.broadcasted_iota(jnp.int32, (256, 128), 1)
    at_edge = ((row + 4) & 127) == (col & 7)
    pick_s[...] = jnp.where(at_edge & (((col >> 3) & 1) == (row >> 7)), 1.0, 0.0).astype(BF16)
    same[0] = jnp.where((row & 7) == (col & 7), 1.0, 0.0).astype(BF16)
    same[1] = jnp.where(at_edge, 1.0, 0.0).astype(BF16)
    for i, shift in enumerate((-1, 0, 1)):
        moves[i] = jnp.where((col & 7) == (row & 7) + shift, 1.0, 0.0).astype(BF16)

    lane = lax.broadcasted_iota(jnp.int32, (64, 128), 1)
    sub = lax.broadcasted_iota(jnp.int32, (64, 128), 0)
    lane8 = lax.broadcasted_iota(jnp.int32, (8, 128), 1)
    low, low8 = (lane & 7) < 4, (lane8 & 7) < 4

    def pick_edges(blocks):
        both = jnp.concatenate(
            [blocks[:, 0].reshape(512, 128), blocks[:, 1].reshape(512, 128)], axis=1
        )
        found = jnp.dot(both, pick_s[...], preferred_element_type=F32)
        total = found[0:64]
        for p in range(1, 8):
            total = jnp.where((lane >> 4) == p, found[64 * p : 64 * p + 64], total)
        return total

    def edges_of(field, parts):
        total = jnp.zeros((64, 128), F32)
        for part in split(field, parts):
            total = total + jnp.dot(part, same[1, :128], preferred_element_type=F32)
        return spread(total)

    loads[0].wait()
    field = av[...]
    out_a[...] = edges_of(field, 3)
    loads[1].wait()
    picked = {8: pick_edges(dv[...])}

    def pick(slots):
        for k in slots:
            load(k).wait()
        for k in slots:
            picked[k] = pick_edges(bv[k])

    def pair(first, second):
        return jnp.where(low, picked[first], pltpu.roll(picked[second], 4, 1))

    def pair_high(first, second):
        return jnp.where(low, pltpu.roll(picked[first], 124, 1), picked[second])

    ghost = lane & 7

    def three(slots, at):
        total = jnp.where(ghost < 2, pltpu.roll(picked[slots[0]], (128 - at) % 128, 1), 0.0)
        for n in (1, 2):
            moved = pltpu.roll(picked[slots[n]], (128 + 2 * n - at) % 128, 1)
            total = jnp.where((ghost >> 1) == n, moved, total)
        return total

    towards, level, away = SLOTS[0]
    pick(towards)
    out_b[0, 0] = pair(towards[0], towards[1]).astype(BF16)
    out_b[0, 1] = pair(towards[2], 8).astype(BF16)
    pl.semaphore_wait(
        barrier, 1 + has_above.astype(jnp.int32) + has_below.astype(jnp.int32)
    )

    ghosts = []
    for side, target in ((0, right), (1, left)):
        for part, (src, dst) in enumerate(
            (
                (out_a, ghost_a.at[1, side]),
                (out_b.at[side, 0:2], ghost_b.at[1, side, 0:2]),
                (out_b.at[side, 2:4], ghost_b.at[1, side, 2:4]),
            )
        ):
            ghosts.append(
                pltpu.make_async_remote_copy(
                    src_ref=src,
                    dst_ref=dst,
                    send_sem=gsend.at[side, part],
                    recv_sem=grecv.at[side, part],
                    device_id=target,
                    device_id_type=MESH,
                )
            )
    ghosts[1].start()
    ghosts[0].start()
    pick(level + away)
    out_b[0, 2] = pair(*level).astype(BF16)
    out_b[0, 3] = three(away, 2).astype(BF16)
    ghosts[2].start()
    for k in range(9):
        edge_b[1, k] = picked[k].astype(BF16)
    towards, level, away = SLOTS[1]
    out_b[1, 0] = pair_high(towards[0], towards[1]).astype(BF16)
    out_b[1, 1] = pair_high(towards[2], 8).astype(BF16)
    out_b[1, 2] = pair_high(*level).astype(BF16)
    out_b[1, 3] = three(away, 4).astype(BF16)

    def along(src, dst, slot, way):
        return pltpu.make_async_remote_copy(
            src_ref=src,
            dst_ref=dst,
            send_sem=asend.at[slot, way],
            recv_sem=arecv.at[slot, way],
            device_id=below if way == 0 else above,
            device_id_type=MESH,
        )

    def rows_copy(step, way):
        return along(ax_out.at[step, way], ax_in.at[step, way], step, way)

    def blocks_copy(way):
        return along(edge_b.at[1], edge_b.at[2 * way], STEPS, way)

    def weighted_copy(way):
        return along(edge_w.at[1], edge_w.at[2 * way], STEPS + 1, way)

    def forward_copy(side, part, way):
        ref = (ghost_a, ghost_b, ghost_b)[part]
        at = ((), (slice(0, 2),), (slice(2, 4),))[part]
        return along(
            ref.at[(1, side) + at],
            ref.at[(2 * way, side) + at],
            STEPS + 2 + 3 * side + part,
            way,
        )

    def forward_copies(side, way):
        return [forward_copy(side, part, way) for part in range(3)]

    def start(copies):
        for way, there in ((0, has_below), (1, has_above)):

            @pl.when(there)
            def _(way=way):
                for copy in copies(way):
                    copy.start()

    def arrive(copies):
        for way, there in ((0, has_above), (1, has_below)):

            @pl.when(there)
            def _(way=way):
                for copy in copies(way):
                    copy.wait_recv()

    def sent(copies):
        for way, there in ((0, has_below), (1, has_above)):

            @pl.when(there)
            def _(way=way):
                for copy in copies(way):
                    copy.wait_send()

    def pass_on(side):
        for part in (1, 0, 2):
            ghosts[3 * side + part].wait_recv()
            if part != 1:
                parts = (0, 1) if part == 0 else (2,)
                start(lambda way: [forward_copy(side, n, way) for n in parts])
        if side == 0:
            for copy in ghosts[3:]:
                copy.start()

    for step in range(STEPS):
        rows = halves(field)
        w = jnp.zeros((64, 128), F32)
        for r in range(16):
            w = w + times(dv[r // 2, r % 2].astype(F32), rows[r])
        source[...] = w if step == 0 else source[...] + w
        rows = halves(w)

        @pl.loop(0, 8)
        def _(k):
            total = jnp.zeros((64, 128), F32)
            for r in range(16):
                total = total + times(bv[k, r // 2, r % 2].astype(F32), rows[r])
            pk[k] = total

        def gathered(slot_left, slot_same, slot_right):
            main = jnp.where(lane == 127, 0.0, pltpu.roll(pk[slot_left], 127, 1))
            main = main + jnp.where(lane == 0, 0.0, pltpu.roll(pk[slot_right], 1, 1))
            return main if slot_same is None else main + pk[slot_same]

        up = gathered(0, 1, 2)
        down = gathered(5, 6, 7)
        up_s[...] = up
        down_s[...] = down
        ax_out[step, 1] = up_s[pl.ds(0, 16, stride=4)]
        ax_out[step, 0] = down_s[pl.ds(3, 16, stride=4)]
        start(lambda way, step=step: [rows_copy(step, way)])
        if step == 0:
            start(lambda way: [blocks_copy(way)])
        if step < STEPS - 1:
            edge_w[1, step] = edges_of(w, 2)
        if step == STEPS - 2:
            start(lambda way: [weighted_copy(way)])
        lifted = pltpu.roll(up.reshape(8, 8, 128), 7, 1).reshape(64, 128)
        dropped = pltpu.roll(down.reshape(8, 8, 128), 1, 1).reshape(64, 128)
        q[...] = (
            gathered(3, None, 4)
            + jnp.where((sub & 3) == 3, 0.0, lifted)
            + jnp.where((sub & 3) == 0, 0.0, dropped)
        )
        if step == STEPS - 2:

            @pl.when(circ > 0)
            def _():
                pass_on(0)

        if step == STEPS - 1:
            pass_on(1)

            @pl.when(circ == 0)
            def _():
                pass_on(0)

        arrive(lambda way, step=step: [rows_copy(step, way)])
        q[pl.ds(0, 16, stride=4)] = q[pl.ds(0, 16, stride=4)] + ax_in[step, 0]
        q[pl.ds(3, 16, stride=4)] = q[pl.ds(3, 16, stride=4)] + ax_in[step, 1]
        field = -q[...]

    def assemble(side, block):
        towards, level, away = SLOTS[side]
        parts = [ghost_b[block, side, n].astype(F32) for n in range(4)]

        def put(to, k, part, by):
            found = pltpu.roll(parts[part], by % 128, 1) if by else parts[part]
            mine = edge_b[block, k].astype(F32)
            to[...] = jnp.where(low if side == 0 else ~low, found, mine)

        base = 4 * side
        for n, k in enumerate(towards):
            put(strip_b.at[side, block, k], k, n // 2, base - 4 * (n % 2))
        put(strip_d.at[side, block], 8, 1, base - 4)
        for n, k in enumerate(level):
            put(strip_b.at[side, block, k], k, 2, base - 4 * n)
        for n, k in enumerate(away):
            put(strip_b.at[side, block, k], k, 3, (2 if side == 0 else 4) - 2 * n)

    def strip(side):
        assemble(side, 1)
        arrive(lambda way: forward_copies(side, way))
        assemble(side, 0)
        assemble(side, 2)
        blocks = range(3)
        outward = (0, 3, 5) if side == 0 else (2, 4, 7)
        crossing = (lane8 & 7) == (4 if side == 0 else 3)
        d, added = None, None
        for step in range(STEPS):
            if step == 0:
                fields = [ghost_a[block, side] for block in blocks]
                if side == 0:
                    fields = [jnp.where(low8, a, 0.0) for a in fields]
                else:
                    fields = [jnp.where(low8, 0.0, a) for a in fields]
            else:
                fields = [spread(x) for x in d]
            p = [times(strip_d[side, block], fields[block]) for block in blocks]
            w = jnp.dot(
                jnp.concatenate(split(jnp.concatenate(p, axis=0), 2), axis=1),
                same[0],
                preferred_element_type=F32,
            )
            added = w[64:128] if step == 0 else added + w[64:128]
            rows = [spread(w[64 * block : 64 * block + 64]) for block in blocks]
            rows_out = rows
            if step < STEPS - 1:
                rows_out = [
                    rows[block] + jnp.where(crossing, edge_w[block, step], 0.0)
                    for block in blocks
                ]

            def flow(k, block):
                return times(
                    strip_b[side, block, k], (rows_out if k in outward else rows)[block]
                )

            def turned(x, by):
                return pltpu.roll(x.reshape(8, 8, 128), by, 1).reshape(64, 128)

            targets = blocks if step < STEPS - 1 else (1,)
            moved = jnp.zeros((64 * len(targets), 128), F32)
            for i, (k_up, k_level, k_down) in enumerate(((0, 3, 5), (1, None, 6), (2, 4, 7))):
                ups = {block: flow(k_up, block) for block in blocks}
                downs = {block: flow(k_down, block) for block in blocks}
                sums = []
                for block in targets:
                    total = turned(ups[block], 7)
                    over = turned(ups[block + 1], 3) if block < 2 else 0.0
                    total = jnp.where((sub & 3) == 3, over, total)
                    falling = turned(downs[block], 1)
                    over = turned(downs[block - 1], 5) if block > 0 else 0.0
                    total = total + jnp.where((sub & 3) == 0, over, falling)
                    if k_level is not None:
                        total = total + flow(k_level, block)
                    sums.append(total)
                moved = moved + jnp.dot(
                    jnp.concatenate(split(jnp.concatenate(sums, axis=0), 2), axis=1),
                    moves[i],
                    preferred_element_type=F32,
                )
            d = [-moved[64 * n : 64 * n + 64] for n in range(len(targets))]
        return added, d[0]

    arrive(lambda way: [blocks_copy(way)])
    arrive(lambda way: [weighted_copy(way)])
    added_right, d_right = strip(1)
    added_left, d_left = strip(0)

    def with_strips(u, left_strip, right_strip):
        u = u + jnp.where(lane < 4, pltpu.roll(left_strip, 124, 1), 0.0)
        return u + jnp.where(lane >= 124, pltpu.roll(right_strip, 4, 1), 0.0)

    source_out[...] = with_strips(source[...], added_left, added_right)
    initial_out[...] = with_strips(field, d_left, d_right)
    for copy in ghosts:
        copy.wait_send()
    for step in range(STEPS):
        sent(lambda way, step=step: [rows_copy(step, way)])
    sent(lambda way: [blocks_copy(way), weighted_copy(way)])
    for side in range(2):
        sent(lambda way, side=side: forward_copies(side, way))


def written(source, initial, source_out, initial_out):
    source_out[...] = source[...]
    initial_out[...] = initial[...]


def per_device(cotangent, off_blocks, diag_inverse):
    vmem, dma = pltpu.VMEM, pltpu.SemaphoreType.DMA
    anywhere = pl.BlockSpec(memory_space=pl.ANY)
    hbm = pl.BlockSpec(memory_space=pltpu.HBM)
    source, initial = pl.pallas_call(
        kernel,
        out_shape=[pltpu.VMEM((64, 128), F32)] * 2,
        in_specs=[hbm] * 3,
        out_specs=[pl.BlockSpec(memory_space=vmem)] * 2,
        scratch_shapes=[
            vmem((64, 128), F32),
            vmem((8, 8, 2, 64, 128), BF16),
            vmem((8, 2, 64, 128), BF16),
            vmem((64, 128), F32),
            vmem((3, 9, 64, 128), BF16),
            vmem((3, 2, 4, 64, 128), BF16),
            vmem((3, 2, 8, 128), F32),
            vmem((2, 4, 64, 128), BF16),
            vmem((8, 128), F32),
            vmem((3, STEPS - 1, 8, 128), F32),
            vmem((2, 3, 8, 64, 128), F32),
            vmem((2, 3, 64, 128), F32),
            vmem((8, 64, 128), F32),
            vmem((64, 128), F32),
            vmem((64, 128), F32),
            vmem((64, 128), F32),
            vmem((STEPS, 2, 16, 128), F32),
            vmem((STEPS, 2, 16, 128), F32),
            vmem((256, 128), BF16),
            vmem((2, 256, 128), BF16),
            vmem((3, 256, 128), BF16),
            dma((10,)),
            dma((2, 3)),
            dma((2, 3)),
            dma((STEPS + 8, 2)),
            dma((STEPS + 8, 2)),
        ],
        compiler_params=pltpu.CompilerParams(
            collective_id=0, has_side_effects=True, vmem_limit_bytes=60 << 20
        ),
        cost_estimate=pl.CostEstimate(
            flops=10 << 20, bytes_accessed=5 << 19, transcendentals=0
        ),
    )(
        cotangent.reshape(64, 128),
        off_blocks.reshape(8, 8, 2, 64, 128),
        diag_inverse.reshape(8, 2, 64, 128),
    )
    source, initial = pl.pallas_call(
        written,
        out_shape=[jax.ShapeDtypeStruct((64, 128), F32)] * 2,
        in_specs=[pl.BlockSpec(memory_space=vmem)] * 2,
        out_specs=[pl.BlockSpec(memory_space=vmem)] * 2,
    )(
        pltpu.with_memory_space_constraint(source, vmem),
        pltpu.with_memory_space_constraint(initial, vmem),
    )
    return source.reshape(cotangent.shape), initial.reshape(cotangent.shape)


def solution(mesh):
    return jax.shard_map(
        per_device,
        mesh=mesh,
        in_specs=(
            P(None, "ax", "circ"),
            P(None, None, None, "ax", "circ"),
            P(None, None, "ax", "circ"),
        ),
        out_specs=(P(None, "ax", "circ"), P(None, "ax", "circ")),
        check_vma=False,
    )
```

```python
import functools

import jax
import jax.numpy as jnp
from jax import lax
from jax.experimental import pallas as pl
from jax.experimental.pallas import tpu as pltpu
from jax.sharding import PartitionSpec as P

STEPS = 4
MESH = pl.DeviceIdType.MESH
F32 = jnp.float32
BF16 = jnp.bfloat16

SLOTS = (((2, 4, 7), (1, 6), (0, 3, 5)), ((0, 3, 5), (1, 6), (2, 4, 7)))


def halves(field):
    sub = lax.broadcasted_iota(jnp.int32, (8, 128), 0)
    out = []
    for v in range(8):
        here = field[8 * v : 8 * v + 8]
        turned = pltpu.roll(here, 4, 0)
        out.append(jnp.where(sub < 4, here, turned))
        out.append(jnp.where(sub < 4, turned, here))
    return out


def spread(field):
    sub = lax.broadcasted_iota(jnp.int32, (8, 128), 0)
    group = lax.broadcasted_iota(jnp.int32, (8, 128), 1) >> 3
    total = jnp.zeros((8, 128), F32)
    for v in range(8):
        total = jnp.where(group == 2 * v + (sub >> 2), field[8 * v : 8 * v + 8], total)
    return total + pltpu.roll(total, 4, 0)


def split(x, parts):
    out = []
    for _ in range(parts):
        part = x.astype(BF16)
        out.append(part)
        x = x - part.astype(F32)
    return out


def times(blocks, rows):
    return (blocks.reshape(8, 8, 128) * rows[None]).reshape(64, 128)


def kernel(
    cot,
    off,
    diag,
    source_out,
    initial_out,
    av,
    bv,
    dv,
    source,
    edge_b,
    ghost_b,
    ghost_a,
    out_b,
    out_a,
    edge_w,
    strip_b,
    strip_d,
    pk,
    up_s,
    down_s,
    q,
    ax_out,
    ax_in,
    pick_s,
    same,
    moves,
    load_sem,
    gsend,
    grecv,
    asend,
    arecv,
):
    ax, circ = lax.axis_index("ax"), lax.axis_index("circ")
    n_ax, n_circ = lax.axis_size("ax"), lax.axis_size("circ")
    right = (ax, lax.rem(circ + 1, n_circ))
    left = (ax, lax.rem(circ + n_circ - 1, n_circ))
    above, below = (ax - 1, circ), (ax + 1, circ)
    has_above, has_below = ax > 0, ax < n_ax - 1

    loads = [
        pltpu.make_async_copy(cot, av, load_sem.at[8]),
        pltpu.make_async_copy(diag, dv, load_sem.at[9]),
    ]
    for copy in loads:
        copy.start()

    def load(k):
        return pltpu.make_async_copy(off.at[k], bv.at[k], load_sem.at[k])

    for group in SLOTS[0]:
        for k in group:
            load(k).start()

    barrier = pltpu.get_barrier_semaphore()

    for way, there in ((0, has_above), (1, has_below)):

        @pl.when(jnp.logical_not(there))
        def _(way=way):
            ax_in[:, way] = jnp.zeros((STEPS, 16, 128), F32)
            edge_b[2 * way] = jnp.zeros((9, 64, 128), BF16)
            ghost_b[2 * way] = jnp.zeros((2, 4, 64, 128), BF16)
            ghost_a[2 * way] = jnp.zeros((2, 8, 128), F32)
            edge_w[2 * way] = jnp.zeros((STEPS - 1, 8, 128), F32)

    pl.semaphore_signal(barrier, inc=1, device_id=left, device_id_type=MESH)

    @pl.when(has_above)
    def _():
        pl.semaphore_signal(barrier, inc=1, device_id=above, device_id_type=MESH)

    @pl.when(has_below)
    def _():
        pl.semaphore_signal(barrier, inc=1, device_id=below, device_id_type=MESH)

    row = lax.broadcasted_iota(jnp.int32, (256, 128), 0)
    col = lax.broadcasted_iota(jnp.int32, (256, 128), 1)
    at_edge = ((row + 4) & 127) == (col & 7)
    pick_s[...] = jnp.where(at_edge & (((col >> 3) & 1) == (row >> 7)), 1.0, 0.0).astype(BF16)
    same[0] = jnp.where((row & 7) == (col & 7), 1.0, 0.0).astype(BF16)
    same[1] = jnp.where(at_edge, 1.0, 0.0).astype(BF16)
    for i, shift in enumerate((-1, 0, 1)):
        moves[i] = jnp.where((col & 7) == (row & 7) + shift, 1.0, 0.0).astype(BF16)

    lane = lax.broadcasted_iota(jnp.int32, (64, 128), 1)
    sub = lax.broadcasted_iota(jnp.int32, (64, 128), 0)
    lane8 = lax.broadcasted_iota(jnp.int32, (8, 128), 1)
    low, low8 = (lane & 7) < 4, (lane8 & 7) < 4

    def pick_edges(blocks):
        both = jnp.concatenate(
            [blocks[:, 0].reshape(512, 128), blocks[:, 1].reshape(512, 128)], axis=1
        )
        found = jnp.dot(both, pick_s[...], preferred_element_type=F32)
        total = found[0:64]
        for p in range(1, 8):
            total = jnp.where((lane >> 4) == p, found[64 * p : 64 * p + 64], total)
        return total

    def edges_of(field, parts):
        total = jnp.zeros((64, 128), F32)
        for part in split(field, parts):
            total = total + jnp.dot(part, same[1, :128], preferred_element_type=F32)
        return spread(total)

    loads[0].wait()
    field = av[...]
    out_a[...] = edges_of(field, 3)
    loads[1].wait()
    picked = {8: pick_edges(dv[...])}

    def pick(slots):
        for k in slots:
            load(k).wait()
        for k in slots:
            picked[k] = pick_edges(bv[k])

    def pair(first, second):
        return jnp.where(low, picked[first], pltpu.roll(picked[second], 4, 1))

    def pair_high(first, second):
        return jnp.where(low, pltpu.roll(picked[first], 124, 1), picked[second])

    ghost = lane & 7

    def three(slots, at):
        total = jnp.where(ghost < 2, pltpu.roll(picked[slots[0]], (128 - at) % 128, 1), 0.0)
        for n in (1, 2):
            moved = pltpu.roll(picked[slots[n]], (128 + 2 * n - at) % 128, 1)
            total = jnp.where((ghost >> 1) == n, moved, total)
        return total

    towards, level, away = SLOTS[0]
    pick(towards)
    out_b[0, 0] = pair(towards[0], towards[1]).astype(BF16)
    out_b[0, 1] = pair(towards[2], 8).astype(BF16)
    pl.semaphore_wait(
        barrier, 1 + has_above.astype(jnp.int32) + has_below.astype(jnp.int32)
    )

    ghosts = []
    for side, target in ((0, right), (1, left)):
        for part, (src, dst) in enumerate(
            (
                (out_a, ghost_a.at[1, side]),
                (out_b.at[side, 0:2], ghost_b.at[1, side, 0:2]),
                (out_b.at[side, 2:4], ghost_b.at[1, side, 2:4]),
            )
        ):
            ghosts.append(
                pltpu.make_async_remote_copy(
                    src_ref=src,
                    dst_ref=dst,
                    send_sem=gsend.at[side, part],
                    recv_sem=grecv.at[side, part],
                    device_id=target,
                    device_id_type=MESH,
                )
            )
    gives_way = circ == n_circ - 3

    @pl.when(jnp.logical_not(gives_way))
    def _():
        ghosts[1].start()
        ghosts[0].start()

    pick(level + away)
    out_b[0, 2] = pair(*level).astype(BF16)
    out_b[0, 3] = three(away, 2).astype(BF16)

    @pl.when(jnp.logical_not(gives_way))
    def _():
        ghosts[2].start()

    for k in range(9):
        edge_b[1, k] = picked[k].astype(BF16)
    towards, level, away = SLOTS[1]
    out_b[1, 0] = pair_high(towards[0], towards[1]).astype(BF16)
    out_b[1, 1] = pair_high(towards[2], 8).astype(BF16)
    out_b[1, 2] = pair_high(*level).astype(BF16)
    out_b[1, 3] = three(away, 4).astype(BF16)

    def along(src, dst, slot, way):
        return pltpu.make_async_remote_copy(
            src_ref=src,
            dst_ref=dst,
            send_sem=asend.at[slot, way],
            recv_sem=arecv.at[slot, way],
            device_id=below if way == 0 else above,
            device_id_type=MESH,
        )

    def rows_copy(step, way):
        return along(ax_out.at[step, way], ax_in.at[step, way], step, way)

    def blocks_copy(way):
        return along(edge_b.at[1], edge_b.at[2 * way], STEPS, way)

    def weighted_copy(way):
        return along(edge_w.at[1], edge_w.at[2 * way], STEPS + 1, way)

    def forward_copy(side, part, way):
        ref = (ghost_a, ghost_b, ghost_b)[part]
        at = ((), (slice(0, 2),), (slice(2, 4),))[part]
        return along(
            ref.at[(1, side) + at],
            ref.at[(2 * way, side) + at],
            STEPS + 2 + 3 * side + part,
            way,
        )

    def forward_copies(side, way):
        return [forward_copy(side, part, way) for part in range(3)]

    def start(copies):
        for way, there in ((0, has_below), (1, has_above)):

            @pl.when(there)
            def _(way=way):
                for copy in copies(way):
                    copy.start()

    def arrive(copies):
        for way, there in ((0, has_above), (1, has_below)):

            @pl.when(there)
            def _(way=way):
                for copy in copies(way):
                    copy.wait_recv()

    def sent(copies):
        for way, there in ((0, has_below), (1, has_above)):

            @pl.when(there)
            def _(way=way):
                for copy in copies(way):
                    copy.wait_send()

    def pass_on(side):
        for part in (1, 0, 2):
            ghosts[3 * side + part].wait_recv()
            if part != 1:
                parts = (0, 1) if part == 0 else (2,)
                start(lambda way: [forward_copy(side, n, way) for n in parts])
        if side == 0:
            for copy in ghosts[3:]:
                copy.start()

    for step in range(STEPS):
        rows = halves(field)
        w = jnp.zeros((64, 128), F32)
        for r in range(16):
            w = w + times(dv[r // 2, r % 2].astype(F32), rows[r])
        source[...] = w if step == 0 else source[...] + w
        rows = halves(w)

        @pl.loop(0, 8)
        def _(k):
            total = jnp.zeros((64, 128), F32)
            for r in range(16):
                total = total + times(bv[k, r // 2, r % 2].astype(F32), rows[r])
            pk[k] = total

        def gathered(slot_left, slot_same, slot_right):
            main = jnp.where(lane == 127, 0.0, pltpu.roll(pk[slot_left], 127, 1))
            main = main + jnp.where(lane == 0, 0.0, pltpu.roll(pk[slot_right], 1, 1))
            return main if slot_same is None else main + pk[slot_same]

        up = gathered(0, 1, 2)
        down = gathered(5, 6, 7)
        up_s[...] = up
        down_s[...] = down
        ax_out[step, 1] = up_s[pl.ds(0, 16, stride=4)]
        ax_out[step, 0] = down_s[pl.ds(3, 16, stride=4)]
        start(lambda way, step=step: [rows_copy(step, way)])
        if step == 0:
            start(lambda way: [blocks_copy(way)])
        if step < STEPS - 1:
            edge_w[1, step] = edges_of(w, 2)
        if step == STEPS - 2:
            start(lambda way: [weighted_copy(way)])
        lifted = pltpu.roll(up.reshape(8, 8, 128), 7, 1).reshape(64, 128)
        dropped = pltpu.roll(down.reshape(8, 8, 128), 1, 1).reshape(64, 128)
        q[...] = (
            gathered(3, None, 4)
            + jnp.where((sub & 3) == 3, 0.0, lifted)
            + jnp.where((sub & 3) == 0, 0.0, dropped)
        )
        if step == STEPS - 2:

            @pl.when(circ > 0)
            def _():
                pass_on(0)

        if step == STEPS - 1:
            pass_on(1)

            @pl.when(circ == 0)
            def _():
                pass_on(0)

        arrive(lambda way, step=step: [rows_copy(step, way)])
        if step == 0:

            @pl.when(gives_way)
            def _():
                for part in (1, 0, 2):
                    ghosts[part].start()

        q[pl.ds(0, 16, stride=4)] = q[pl.ds(0, 16, stride=4)] + ax_in[step, 0]
        q[pl.ds(3, 16, stride=4)] = q[pl.ds(3, 16, stride=4)] + ax_in[step, 1]
        field = -q[...]

    def assemble(side, block):
        towards, level, away = SLOTS[side]
        parts = [ghost_b[block, side, n].astype(F32) for n in range(4)]

        def put(to, k, part, by):
            found = pltpu.roll(parts[part], by % 128, 1) if by else parts[part]
            mine = edge_b[block, k].astype(F32)
            to[...] = jnp.where(low if side == 0 else ~low, found, mine)

        base = 4 * side
        for n, k in enumerate(towards):
            put(strip_b.at[side, block, k], k, n // 2, base - 4 * (n % 2))
        put(strip_d.at[side, block], 8, 1, base - 4)
        for n, k in enumerate(level):
            put(strip_b.at[side, block, k], k, 2, base - 4 * n)
        for n, k in enumerate(away):
            put(strip_b.at[side, block, k], k, 3, (2 if side == 0 else 4) - 2 * n)

    def strip(side):
        assemble(side, 1)
        arrive(lambda way: forward_copies(side, way))
        assemble(side, 0)
        assemble(side, 2)
        blocks = range(3)
        outward = (0, 3, 5) if side == 0 else (2, 4, 7)
        crossing = (lane8 & 7) == (4 if side == 0 else 3)
        d, added = None, None
        for step in range(STEPS):
            if step == 0:
                fields = [ghost_a[block, side] for block in blocks]
                if side == 0:
                    fields = [jnp.where(low8, a, 0.0) for a in fields]
                else:
                    fields = [jnp.where(low8, 0.0, a) for a in fields]
            else:
                fields = [spread(x) for x in d]
            p = [times(strip_d[side, block], fields[block]) for block in blocks]
            w = jnp.dot(
                jnp.concatenate(split(jnp.concatenate(p, axis=0), 2), axis=1),
                same[0],
                preferred_element_type=F32,
            )
            added = w[64:128] if step == 0 else added + w[64:128]
            rows = [spread(w[64 * block : 64 * block + 64]) for block in blocks]
            rows_out = rows
            if step < STEPS - 1:
                rows_out = [
                    rows[block] + jnp.where(crossing, edge_w[block, step], 0.0)
                    for block in blocks
                ]

            def flow(k, block):
                return times(
                    strip_b[side, block, k], (rows_out if k in outward else rows)[block]
                )

            def turned(x, by):
                return pltpu.roll(x.reshape(8, 8, 128), by, 1).reshape(64, 128)

            targets = blocks if step < STEPS - 1 else (1,)
            moved = []
            for k_up, k_level, k_down in ((0, 3, 5), (1, None, 6), (2, 4, 7)):
                ups = {block: flow(k_up, block) for block in blocks}
                downs = {block: flow(k_down, block) for block in blocks}
                sums = []
                for block in targets:
                    total = turned(ups[block], 7)
                    over = turned(ups[block + 1], 3) if block < 2 else 0.0
                    total = jnp.where((sub & 3) == 3, over, total)
                    falling = turned(downs[block], 1)
                    over = turned(downs[block - 1], 5) if block > 0 else 0.0
                    total = total + jnp.where((sub & 3) == 0, over, falling)
                    if k_level is not None:
                        total = total + flow(k_level, block)
                    sums.append(total)
                moved += split(jnp.concatenate(sums, axis=0), 2)
            moved = jnp.dot(
                jnp.concatenate(moved, axis=1),
                moves[...].reshape(768, 128),
                preferred_element_type=F32,
            )
            d = [-moved[64 * n : 64 * n + 64] for n in range(len(targets))]
        return added, d[0]

    arrive(lambda way: [blocks_copy(way)])
    arrive(lambda way: [weighted_copy(way)])
    added_right, d_right = strip(1)
    for copy in ghosts[:3]:
        copy.wait_send()
    sent(
        lambda way: [rows_copy(step, way) for step in range(STEPS)]
        + [blocks_copy(way), weighted_copy(way)]
        + forward_copies(1, way)
    )
    added_left, d_left = strip(0)

    def with_strips(u, left_strip, right_strip):
        u = u + jnp.where(lane < 4, pltpu.roll(left_strip, 124, 1), 0.0)
        return u + jnp.where(lane >= 124, pltpu.roll(right_strip, 4, 1), 0.0)

    source_out[...] = with_strips(source[...], added_left, added_right)
    initial_out[...] = with_strips(field, d_left, d_right)
    for copy in ghosts[3:]:
        copy.wait_send()
    sent(lambda way: forward_copies(0, way))


def written(source, initial, source_out, initial_out):
    source_out[...] = source[...]
    initial_out[...] = initial[...]


def per_device(cotangent, off_blocks, diag_inverse):
    vmem, dma = pltpu.VMEM, pltpu.SemaphoreType.DMA
    anywhere = pl.BlockSpec(memory_space=pl.ANY)
    hbm = pl.BlockSpec(memory_space=pltpu.HBM)
    source, initial = pl.pallas_call(
        kernel,
        out_shape=[pltpu.VMEM((64, 128), F32)] * 2,
        in_specs=[hbm] * 3,
        out_specs=[pl.BlockSpec(memory_space=vmem)] * 2,
        scratch_shapes=[
            vmem((64, 128), F32),
            vmem((8, 8, 2, 64, 128), BF16),
            vmem((8, 2, 64, 128), BF16),
            vmem((64, 128), F32),
            vmem((3, 9, 64, 128), BF16),
            vmem((3, 2, 4, 64, 128), BF16),
            vmem((3, 2, 8, 128), F32),
            vmem((2, 4, 64, 128), BF16),
            vmem((8, 128), F32),
            vmem((3, STEPS - 1, 8, 128), F32),
            vmem((2, 3, 8, 64, 128), F32),
            vmem((2, 3, 64, 128), F32),
            vmem((8, 64, 128), F32),
            vmem((64, 128), F32),
            vmem((64, 128), F32),
            vmem((64, 128), F32),
            vmem((STEPS, 2, 16, 128), F32),
            vmem((STEPS, 2, 16, 128), F32),
            vmem((256, 128), BF16),
            vmem((2, 256, 128), BF16),
            vmem((3, 256, 128), BF16),
            dma((10,)),
            dma((2, 3)),
            dma((2, 3)),
            dma((STEPS + 8, 2)),
            dma((STEPS + 8, 2)),
        ],
        compiler_params=pltpu.CompilerParams(
            collective_id=0, has_side_effects=True, vmem_limit_bytes=60 << 20
        ),
        cost_estimate=pl.CostEstimate(
            flops=10 << 20, bytes_accessed=5 << 19, transcendentals=0
        ),
    )(
        cotangent.reshape(64, 128),
        off_blocks.reshape(8, 8, 2, 64, 128),
        diag_inverse.reshape(8, 2, 64, 128),
    )
    source, initial = pl.pallas_call(
        written,
        out_shape=[jax.ShapeDtypeStruct((64, 128), F32)] * 2,
        in_specs=[pl.BlockSpec(memory_space=vmem)] * 2,
        out_specs=[pl.BlockSpec(memory_space=vmem)] * 2,
    )(
        pltpu.with_memory_space_constraint(source, vmem),
        pltpu.with_memory_space_constraint(initial, vmem),
    )
    return source.reshape(cotangent.shape), initial.reshape(cotangent.shape)


def solution(mesh):
    return jax.shard_map(
        per_device,
        mesh=mesh,
        in_specs=(
            P(None, "ax", "circ"),
            P(None, None, None, "ax", "circ"),
            P(None, None, "ax", "circ"),
        ),
        out_specs=(P(None, "ax", "circ"), P(None, "ax", "circ")),
        check_vma=False,
    )
```

```python
import functools

import jax
import jax.numpy as jnp
from jax import lax
from jax.experimental import pallas as pl
from jax.experimental.pallas import tpu as pltpu
from jax.sharding import PartitionSpec as P

STEPS = 4
MESH = pl.DeviceIdType.MESH
F32 = jnp.float32
BF16 = jnp.bfloat16

SLOTS = (((2, 4, 7), (1, 6), (0, 3, 5)), ((0, 3, 5), (1, 6), (2, 4, 7)))


def halves(field):
    sub = lax.broadcasted_iota(jnp.int32, (8, 128), 0)
    out = []
    for v in range(8):
        here = field[8 * v : 8 * v + 8]
        turned = pltpu.roll(here, 4, 0)
        out.append(jnp.where(sub < 4, here, turned))
        out.append(jnp.where(sub < 4, turned, here))
    return out


def spread(field):
    sub = lax.broadcasted_iota(jnp.int32, (8, 128), 0)
    group = lax.broadcasted_iota(jnp.int32, (8, 128), 1) >> 3
    total = jnp.zeros((8, 128), F32)
    for v in range(8):
        total = jnp.where(group == 2 * v + (sub >> 2), field[8 * v : 8 * v + 8], total)
    return total + pltpu.roll(total, 4, 0)


def split(x, parts):
    out = []
    for _ in range(parts):
        part = x.astype(BF16)
        out.append(part)
        x = x - part.astype(F32)
    return out


def times(blocks, rows):
    return (blocks.reshape(8, 8, 128) * rows[None]).reshape(64, 128)


def kernel(
    cot,
    off,
    diag,
    source_out,
    initial_out,
    av,
    bv,
    dv,
    source,
    edge_b,
    ghost_b,
    ghost_a,
    out_b,
    out_a,
    edge_w,
    strip_b,
    strip_d,
    pk,
    up_s,
    down_s,
    q,
    ax_out,
    ax_in,
    pick_s,
    same,
    moves,
    load_sem,
    gsend,
    grecv,
    asend,
    arecv,
):
    ax, circ = lax.axis_index("ax"), lax.axis_index("circ")
    n_ax, n_circ = lax.axis_size("ax"), lax.axis_size("circ")
    right = (ax, lax.rem(circ + 1, n_circ))
    left = (ax, lax.rem(circ + n_circ - 1, n_circ))
    above, below = (ax - 1, circ), (ax + 1, circ)
    has_above, has_below = ax > 0, ax < n_ax - 1

    loads = [
        pltpu.make_async_copy(cot, av, load_sem.at[8]),
        pltpu.make_async_copy(diag, dv, load_sem.at[9]),
    ]
    for copy in loads:
        copy.start()

    def load(k):
        return pltpu.make_async_copy(off.at[k], bv.at[k], load_sem.at[k])

    for group in SLOTS[0]:
        for k in group:
            load(k).start()

    barrier = pltpu.get_barrier_semaphore()

    for way, there in ((0, has_above), (1, has_below)):

        @pl.when(jnp.logical_not(there))
        def _(way=way):
            ax_in[:, way] = jnp.zeros((STEPS, 16, 128), F32)
            edge_b[2 * way] = jnp.zeros((9, 64, 128), BF16)
            ghost_b[2 * way] = jnp.zeros((2, 4, 64, 128), BF16)
            ghost_a[2 * way] = jnp.zeros((2, 8, 128), F32)
            edge_w[2 * way] = jnp.zeros((STEPS - 1, 8, 128), F32)

    pl.semaphore_signal(barrier, inc=1, device_id=left, device_id_type=MESH)

    @pl.when(has_above)
    def _():
        pl.semaphore_signal(barrier, inc=1, device_id=above, device_id_type=MESH)

    @pl.when(has_below)
    def _():
        pl.semaphore_signal(barrier, inc=1, device_id=below, device_id_type=MESH)

    row = lax.broadcasted_iota(jnp.int32, (256, 128), 0)
    col = lax.broadcasted_iota(jnp.int32, (256, 128), 1)
    at_edge = ((row + 4) & 127) == (col & 7)
    pick_s[...] = jnp.where(at_edge & (((col >> 3) & 1) == (row >> 7)), 1.0, 0.0).astype(BF16)
    same[0] = jnp.where((row & 7) == (col & 7), 1.0, 0.0).astype(BF16)
    same[1] = jnp.where(at_edge, 1.0, 0.0).astype(BF16)
    for i, shift in enumerate((-1, 0, 1)):
        moves[i] = jnp.where((col & 7) == (row & 7) + shift, 1.0, 0.0).astype(BF16)

    lane = lax.broadcasted_iota(jnp.int32, (64, 128), 1)
    sub = lax.broadcasted_iota(jnp.int32, (64, 128), 0)
    lane8 = lax.broadcasted_iota(jnp.int32, (8, 128), 1)
    low, low8 = (lane & 7) < 4, (lane8 & 7) < 4

    def pick_edges(blocks):
        both = jnp.concatenate(
            [blocks[:, 0].reshape(512, 128), blocks[:, 1].reshape(512, 128)], axis=1
        )
        found = jnp.dot(both, pick_s[...], preferred_element_type=F32)
        total = found[0:64]
        for p in range(1, 8):
            total = jnp.where((lane >> 4) == p, found[64 * p : 64 * p + 64], total)
        return total

    def edges_of(field, parts):
        total = jnp.zeros((64, 128), F32)
        for part in split(field, parts):
            total = total + jnp.dot(part, same[1, :128], preferred_element_type=F32)
        return spread(total)

    loads[0].wait()
    field = av[...]
    out_a[...] = edges_of(field, 3)
    loads[1].wait()
    picked = {8: pick_edges(dv[...])}

    def pick(slots):
        for k in slots:
            load(k).wait()
        for k in slots:
            picked[k] = pick_edges(bv[k])

    def pair(first, second):
        return jnp.where(low, picked[first], pltpu.roll(picked[second], 4, 1))

    def pair_high(first, second):
        return jnp.where(low, pltpu.roll(picked[first], 124, 1), picked[second])

    ghost = lane & 7

    def three(slots, at):
        total = jnp.where(ghost < 2, pltpu.roll(picked[slots[0]], (128 - at) % 128, 1), 0.0)
        for n in (1, 2):
            moved = pltpu.roll(picked[slots[n]], (128 + 2 * n - at) % 128, 1)
            total = jnp.where((ghost >> 1) == n, moved, total)
        return total

    towards, level, away = SLOTS[0]
    pick(towards)
    out_b[0, 0] = pair(towards[0], towards[1]).astype(BF16)
    out_b[0, 1] = pair(towards[2], 8).astype(BF16)
    pl.semaphore_wait(
        barrier, 1 + has_above.astype(jnp.int32) + has_below.astype(jnp.int32)
    )

    ghosts = []
    for side, target in ((0, right), (1, left)):
        for part, (src, dst) in enumerate(
            (
                (out_a, ghost_a.at[1, side]),
                (out_b.at[side, 0:2], ghost_b.at[1, side, 0:2]),
                (out_b.at[side, 2:4], ghost_b.at[1, side, 2:4]),
            )
        ):
            ghosts.append(
                pltpu.make_async_remote_copy(
                    src_ref=src,
                    dst_ref=dst,
                    send_sem=gsend.at[side, part],
                    recv_sem=grecv.at[side, part],
                    device_id=target,
                    device_id_type=MESH,
                )
            )
    gives_way = circ == n_circ - 3

    @pl.when(jnp.logical_not(gives_way))
    def _():
        ghosts[1].start()
        ghosts[0].start()

    pick(level + away)
    out_b[0, 2] = pair(*level).astype(BF16)
    out_b[0, 3] = three(away, 2).astype(BF16)

    @pl.when(jnp.logical_not(gives_way))
    def _():
        ghosts[2].start()

    for k in range(9):
        edge_b[1, k] = picked[k].astype(BF16)
    def along(src, dst, slot, way):
        return pltpu.make_async_remote_copy(
            src_ref=src,
            dst_ref=dst,
            send_sem=asend.at[slot, way],
            recv_sem=arecv.at[slot, way],
            device_id=below if way == 0 else above,
            device_id_type=MESH,
        )

    def rows_copy(step, way):
        return along(ax_out.at[step, way], ax_in.at[step, way], step, way)

    def blocks_copy(way):
        return along(edge_b.at[1], edge_b.at[2 * way], STEPS, way)

    def weighted_copy(way):
        return along(edge_w.at[1], edge_w.at[2 * way], STEPS + 1, way)

    def forward_copy(side, part, way):
        ref = (ghost_a, ghost_b, ghost_b)[part]
        at = ((), (slice(0, 2),), (slice(2, 4),))[part]
        return along(
            ref.at[(1, side) + at],
            ref.at[(2 * way, side) + at],
            STEPS + 2 + 3 * side + part,
            way,
        )

    def forward_copies(side, way):
        return [forward_copy(side, part, way) for part in range(3)]

    def start(copies):
        for way, there in ((0, has_below), (1, has_above)):

            @pl.when(there)
            def _(way=way):
                for copy in copies(way):
                    copy.start()

    def arrive(copies):
        for way, there in ((0, has_above), (1, has_below)):

            @pl.when(there)
            def _(way=way):
                for copy in copies(way):
                    copy.wait_recv()

    def sent(copies):
        for way, there in ((0, has_below), (1, has_above)):

            @pl.when(there)
            def _(way=way):
                for copy in copies(way):
                    copy.wait_send()

    def pass_on(side):
        for part in (1, 0, 2):
            ghosts[3 * side + part].wait_recv()
            if part != 1:
                parts = (0, 1) if part == 0 else (2,)
                start(lambda way: [forward_copy(side, n, way) for n in parts])
        if side == 0:
            for copy in ghosts[3:]:
                copy.start()

    for step in range(STEPS):
        rows = halves(field)
        w = jnp.zeros((64, 128), F32)
        for r in range(16):
            w = w + times(dv[r // 2, r % 2].astype(F32), rows[r])
        source[...] = w if step == 0 else source[...] + w
        rows = halves(w)

        @pl.loop(0, 8)
        def _(k):
            total = jnp.zeros((64, 128), F32)
            for r in range(16):
                total = total + times(bv[k, r // 2, r % 2].astype(F32), rows[r])
            pk[k] = total

        def gathered(slot_left, slot_same, slot_right):
            main = jnp.where(lane == 127, 0.0, pltpu.roll(pk[slot_left], 127, 1))
            main = main + jnp.where(lane == 0, 0.0, pltpu.roll(pk[slot_right], 1, 1))
            return main if slot_same is None else main + pk[slot_same]

        up = gathered(0, 1, 2)
        down = gathered(5, 6, 7)
        up_s[...] = up
        down_s[...] = down
        ax_out[step, 1] = up_s[pl.ds(0, 16, stride=4)]
        ax_out[step, 0] = down_s[pl.ds(3, 16, stride=4)]
        start(lambda way, step=step: [rows_copy(step, way)])
        if step == 0:
            start(lambda way: [blocks_copy(way)])
            for k in range(9):
                picked[k] = edge_b[1, k].astype(F32)
            towards, level, away = SLOTS[1]
            out_b[1, 0] = pair_high(towards[0], towards[1]).astype(BF16)
            out_b[1, 1] = pair_high(towards[2], 8).astype(BF16)
            out_b[1, 2] = pair_high(*level).astype(BF16)
            out_b[1, 3] = three(away, 4).astype(BF16)
        if step < STEPS - 1:
            edge_w[1, step] = edges_of(w, 2)
        if step == STEPS - 2:
            start(lambda way: [weighted_copy(way)])
        lifted = pltpu.roll(up.reshape(8, 8, 128), 7, 1).reshape(64, 128)
        dropped = pltpu.roll(down.reshape(8, 8, 128), 1, 1).reshape(64, 128)
        q[...] = (
            gathered(3, None, 4)
            + jnp.where((sub & 3) == 3, 0.0, lifted)
            + jnp.where((sub & 3) == 0, 0.0, dropped)
        )
        if step == STEPS - 2:

            @pl.when(circ > 0)
            def _():
                pass_on(0)

        if step == STEPS - 1:
            pass_on(1)

            @pl.when(circ == 0)
            def _():
                pass_on(0)

        arrive(lambda way, step=step: [rows_copy(step, way)])
        if step == 0:

            @pl.when(gives_way)
            def _():
                for part in (1, 0, 2):
                    ghosts[part].start()

        q[pl.ds(0, 16, stride=4)] = q[pl.ds(0, 16, stride=4)] + ax_in[step, 0]
        q[pl.ds(3, 16, stride=4)] = q[pl.ds(3, 16, stride=4)] + ax_in[step, 1]
        field = -q[...]

    def assemble(side, block):
        towards, level, away = SLOTS[side]
        parts = [ghost_b[block, side, n].astype(F32) for n in range(4)]

        def put(to, k, part, by):
            found = pltpu.roll(parts[part], by % 128, 1) if by else parts[part]
            mine = edge_b[block, k].astype(F32)
            to[...] = jnp.where(low if side == 0 else ~low, found, mine)

        base = 4 * side
        for n, k in enumerate(towards):
            put(strip_b.at[side, block, k], k, n // 2, base - 4 * (n % 2))
        put(strip_d.at[side, block], 8, 1, base - 4)
        for n, k in enumerate(level):
            put(strip_b.at[side, block, k], k, 2, base - 4 * n)
        for n, k in enumerate(away):
            put(strip_b.at[side, block, k], k, 3, (2 if side == 0 else 4) - 2 * n)

    def strip(side):
        assemble(side, 1)
        arrive(lambda way: forward_copies(side, way))
        assemble(side, 0)
        assemble(side, 2)
        blocks = range(3)
        outward = (0, 3, 5) if side == 0 else (2, 4, 7)
        crossing = (lane8 & 7) == (4 if side == 0 else 3)
        d, added = None, None
        for step in range(STEPS):
            if step == 0:
                fields = [ghost_a[block, side] for block in blocks]
                if side == 0:
                    fields = [jnp.where(low8, a, 0.0) for a in fields]
                else:
                    fields = [jnp.where(low8, 0.0, a) for a in fields]
            else:
                fields = [spread(x) for x in d]
            p = [times(strip_d[side, block], fields[block]) for block in blocks]
            w = jnp.dot(
                jnp.concatenate(split(jnp.concatenate(p, axis=0), 2), axis=1),
                same[0],
                preferred_element_type=F32,
            )
            added = w[64:128] if step == 0 else added + w[64:128]
            rows = [spread(w[64 * block : 64 * block + 64]) for block in blocks]
            rows_out = rows
            if step < STEPS - 1:
                rows_out = [
                    rows[block] + jnp.where(crossing, edge_w[block, step], 0.0)
                    for block in blocks
                ]

            def flow(k, block):
                return times(
                    strip_b[side, block, k], (rows_out if k in outward else rows)[block]
                )

            def turned(x, by):
                return pltpu.roll(x.reshape(8, 8, 128), by, 1).reshape(64, 128)

            targets = blocks if step < STEPS - 1 else (1,)
            moved = []
            for k_up, k_level, k_down in ((0, 3, 5), (1, None, 6), (2, 4, 7)):
                ups = {block: flow(k_up, block) for block in blocks}
                downs = {block: flow(k_down, block) for block in blocks}
                sums = []
                for block in targets:
                    total = turned(ups[block], 7)
                    over = turned(ups[block + 1], 3) if block < 2 else 0.0
                    total = jnp.where((sub & 3) == 3, over, total)
                    falling = turned(downs[block], 1)
                    over = turned(downs[block - 1], 5) if block > 0 else 0.0
                    total = total + jnp.where((sub & 3) == 0, over, falling)
                    if k_level is not None:
                        total = total + flow(k_level, block)
                    sums.append(total)
                moved += split(jnp.concatenate(sums, axis=0), 2)
            moved = jnp.dot(
                jnp.concatenate(moved, axis=1),
                moves[...].reshape(768, 128),
                preferred_element_type=F32,
            )
            d = [-moved[64 * n : 64 * n + 64] for n in range(len(targets))]
        return added, d[0]

    arrive(lambda way: [blocks_copy(way)])
    arrive(lambda way: [weighted_copy(way)])
    added_right, d_right = strip(1)
    for copy in ghosts[:3]:
        copy.wait_send()
    sent(
        lambda way: [rows_copy(step, way) for step in range(STEPS)]
        + [blocks_copy(way), weighted_copy(way)]
        + forward_copies(1, way)
    )
    added_left, d_left = strip(0)

    def with_strips(u, left_strip, right_strip):
        u = u + jnp.where(lane < 4, pltpu.roll(left_strip, 124, 1), 0.0)
        return u + jnp.where(lane >= 124, pltpu.roll(right_strip, 4, 1), 0.0)

    source_out[...] = with_strips(source[...], added_left, added_right)
    initial_out[...] = with_strips(field, d_left, d_right)
    for copy in ghosts[3:]:
        copy.wait_send()
    sent(lambda way: forward_copies(0, way))


def written(source, initial, source_out, initial_out):
    source_out[...] = source[...]
    initial_out[...] = initial[...]


def per_device(cotangent, off_blocks, diag_inverse):
    vmem, dma = pltpu.VMEM, pltpu.SemaphoreType.DMA
    anywhere = pl.BlockSpec(memory_space=pl.ANY)
    hbm = pl.BlockSpec(memory_space=pltpu.HBM)
    source, initial = pl.pallas_call(
        kernel,
        out_shape=[pltpu.VMEM((64, 128), F32)] * 2,
        in_specs=[hbm] * 3,
        out_specs=[pl.BlockSpec(memory_space=vmem)] * 2,
        scratch_shapes=[
            vmem((64, 128), F32),
            vmem((8, 8, 2, 64, 128), BF16),
            vmem((8, 2, 64, 128), BF16),
            vmem((64, 128), F32),
            vmem((3, 9, 64, 128), BF16),
            vmem((3, 2, 4, 64, 128), BF16),
            vmem((3, 2, 8, 128), F32),
            vmem((2, 4, 64, 128), BF16),
            vmem((8, 128), F32),
            vmem((3, STEPS - 1, 8, 128), F32),
            vmem((2, 3, 8, 64, 128), F32),
            vmem((2, 3, 64, 128), F32),
            vmem((8, 64, 128), F32),
            vmem((64, 128), F32),
            vmem((64, 128), F32),
            vmem((64, 128), F32),
            vmem((STEPS, 2, 16, 128), F32),
            vmem((STEPS, 2, 16, 128), F32),
            vmem((256, 128), BF16),
            vmem((2, 256, 128), BF16),
            vmem((3, 256, 128), BF16),
            dma((10,)),
            dma((2, 3)),
            dma((2, 3)),
            dma((STEPS + 8, 2)),
            dma((STEPS + 8, 2)),
        ],
        compiler_params=pltpu.CompilerParams(
            collective_id=0, has_side_effects=True, vmem_limit_bytes=60 << 20
        ),
        cost_estimate=pl.CostEstimate(
            flops=10 << 20, bytes_accessed=5 << 19, transcendentals=0
        ),
    )(
        cotangent.reshape(64, 128),
        off_blocks.reshape(8, 8, 2, 64, 128),
        diag_inverse.reshape(8, 2, 64, 128),
    )
    source, initial = pl.pallas_call(
        written,
        out_shape=[jax.ShapeDtypeStruct((64, 128), F32)] * 2,
        in_specs=[pl.BlockSpec(memory_space=vmem)] * 2,
        out_specs=[pl.BlockSpec(memory_space=vmem)] * 2,
    )(
        pltpu.with_memory_space_constraint(source, vmem),
        pltpu.with_memory_space_constraint(initial, vmem),
    )
    return source.reshape(cotangent.shape), initial.reshape(cotangent.shape)


def solution(mesh):
    return jax.shard_map(
        per_device,
        mesh=mesh,
        in_specs=(
            P(None, "ax", "circ"),
            P(None, None, None, "ax", "circ"),
            P(None, None, "ax", "circ"),
        ),
        out_specs=(P(None, "ax", "circ"), P(None, "ax", "circ")),
        check_vma=False,
    )
```
